256 devices in a mesh: head: 16 (over y, x), ctx: 16 (over z, core).
Axes of the slice: x: 4, y: 4, z: 8, core: 2. Of those that a mesh axis runs over, the one named last changes fastest.
Arguments:
- queries: bfloat16 [256, 128, 576], P('head'), may hold values from -41 to 41
- cache: bfloat16 [32768, 576], P('ctx'), may hold values from -11 to 11
- cache_len: int32 [16], P('ctx'), may hold values from 1 to 2048, 24576 in all
- span_start: int32 [1], replicated, may hold values from 28672 to 32512
- value_up: bfloat16 [128, 512, 128], P('head'), may hold values from -0.25 to 0.25
Outputs:
- attended: bfloat16 [256, 128, 128], P('ctx', 'head')
The draws below stay inside these ranges and needn't reach their ends.
Inputs may be any that keep to these rules, and one draw needn't show every extreme that they name: Shard c holds cache_len[c] filled slots at its start; some shard is full.
All inputs are finite; a program needn't handle non-finite values.
Results may differ from the reference program's by a relative error of at most 0.01.
Values may be sent and summed in bfloat16 or wider, within the bound.
No kernel may reach another device: no remote copies, remote signals or barrier semaphores. Data moves between devices by JAX's collectives and lax.ppermute only.
A program may use at most 128 MiB of HBM per device.

```python
import math
import jax
import jax.numpy as jnp
import numpy as np
from jax import lax

H = 128
DC = 512
DR = 64
NOPE = 128
DV = 128
S = 256
CTX_DEV = 2048
CTXLEN = 32768
N_CTX = 16


def latent_base(key):
    return jnp.clip(jax.random.normal(key, (CTXLEN, DC + DR), jnp.float32), -5.0, 5.0)


def draw_cache(key, part):
    base = latent_base(key)
    cache = base
    return cache.astype(jnp.bfloat16)


def draw_queries(key, part):
    key = jax.random.fold_in(key, 23)
    fresh = jnp.clip(jax.random.normal(key, (S, H, DC + DR), jnp.float32), -6.0, 6.0)
    return fresh.astype(jnp.bfloat16)


def level_of(own_key, extent, pieces, least, high):
    level = 1.0
    for dim, parts in pieces:
        draws = jax.random.uniform(jax.random.fold_in(jax.random.fold_in(own_key, 6), dim), (parts,), jnp.float32, least / len(pieces), high / len(pieces))
        level = level * jnp.repeat(jnp.exp(draws), extent[dim] // parts).reshape((-1,) + (1,) * (len(extent) - 1 - dim))
    return level


def split_up(amount, total, bound, skew):
    weights = [(1 << 20) // math.isqrt(standing ** skew) + 1 for standing in range(2, amount + 1)]
    spare, counts = total - bound - (amount - 1), [1] * (amount - 1)
    while spare > 0:
        free = [i for i in range(amount - 1) if counts[i] < bound]
        pool, remaining = sum([weights[i] for i in free]), spare
        for i in free:
            more = min(bound - counts[i], max(1, remaining * weights[i] // pool), spare)
            counts[i] = counts[i] + more
            spare = spare - more
    return np.array([bound] + counts)


def uneven_parts(rng, number_of, total, bound, slope):
    if number_of == 2:
        one = jax.random.randint(rng, (), max(1, total - bound), min(bound, total - 1) + 1)
        return jnp.stack([one, total - one])
    tallies = jnp.asarray(split_up(number_of, total, bound, slope), jnp.int32)
    twos = (number_of - 1) // 2
    source_of, taker = tallies[1:1 + 2 * twos:2], tallies[2:2 + 2 * twos:2]
    margin = jnp.minimum(source_of - 1, bound - taker)
    shifted = jax.random.randint(jax.random.fold_in(rng, 1), (twos,), 0, 1 << 20) % (margin + 1)
    tallies = tallies.at[1:1 + 2 * twos:2].set(source_of - shifted).at[2:2 + 2 * twos:2].set(taker + shifted)
    return tallies[jax.random.permutation(jax.random.fold_in(rng, 2), number_of)]


def scatter_about(key, extent, deviation, bound, split=(), held_as=jnp.bfloat16):
    result = jax.random.normal(key, extent, jnp.float32) * deviation
    if len(split) > 0:
        result = level_of(key, extent, split, -0.22, 0.18) * result
    return jnp.clip(result, min=-bound, max=bound).astype(held_as)


def setup_inputs(seed: int = 0) -> dict:
    key_list = jax.random.split(jax.random.key(seed), 6)
    return {
        "queries": draw_queries(jax.random.fold_in(key_list[5], 71), 0),
        "cache": draw_cache(jax.random.fold_in(key_list[5], 71), 0),
        "cache_len": uneven_parts(key_list[2], N_CTX, 3 * CTX_DEV * N_CTX // 4, CTX_DEV, 1).astype(jnp.int32),
        "span_start": jax.random.randint(key_list[3], (1,), (N_CTX - 2) * CTX_DEV, N_CTX * CTX_DEV - S + 1).astype(jnp.int32),
        "value_up": scatter_about(key_list[4], (H, DC, DV), DC ** -0.5, 0.25, ((0, 16),)),
    }


def shard_part(rows, ckv, valid, groups):
    scale = (NOPE + DR) ** -0.5
    scores = jnp.dot(rows, ckv.T, preferred_element_type=jnp.float32) * scale
    scores = scores.reshape(S, groups, ckv.shape[0])
    mask = valid[:, None, :]
    shard_max = jnp.max(jnp.where(mask, scores, jnp.float32(-1e30)), axis=2, keepdims=True)
    weights = jnp.where(mask, jnp.exp(scores - shard_max), jnp.float32(0.0))
    total = jnp.sum(weights, axis=2)
    bounded = jnp.maximum(total, jnp.float32(1.0))
    flat = weights.astype(jnp.bfloat16).reshape(S * groups, ckv.shape[0])
    acc = jnp.dot(flat, ckv[:, :DC], preferred_element_type=jnp.float32).reshape(S, groups, DC)
    partial_value = (acc / bounded[:, :, None]).astype(jnp.bfloat16)
    lse = shard_max[:, :, 0] + jnp.log(bounded)
    return partial_value, lse


def reference(queries, cache, cache_len, span_start, value_up):
    groups = min(8, H)
    count = H // groups
    width = DC + DR
    grouped = queries.reshape(S, count, groups, width).transpose(1, 0, 2, 3)
    ups = value_up.reshape(count, groups, DC, DV)
    limit = span_start[0] + jnp.arange(S, dtype=jnp.int32)
    slots = jnp.arange(CTX_DEV, dtype=jnp.int32)

    def one_group(items):
        block, up = items
        rows = block.reshape(S * groups, width)
        top = jnp.full((S, groups), -1e30, jnp.float32)
        numer = jnp.zeros((S, groups, DC), jnp.float32)
        denom = jnp.zeros((S, groups), jnp.float32)
        for shard in range(N_CTX):
            ckv = cache[shard * CTX_DEV:(shard + 1) * CTX_DEV]
            valid = (slots[None, :] < cache_len[shard]) & (shard * CTX_DEV + slots[None, :] <= limit[:, None])
            partial_value, lse = shard_part(rows, ckv, valid, groups)
            new_top = jnp.maximum(top, lse)
            old_w = jnp.exp(top - new_top)
            new_w = jnp.exp(lse - new_top)
            numer = numer * old_w[:, :, None] + new_w[:, :, None] * partial_value.astype(jnp.float32)
            denom = denom * old_w + new_w
            top = new_top
        merged = numer / denom[:, :, None]
        out = jnp.einsum("sgc,gcv->sgv", merged, up.astype(jnp.float32), precision=lax.Precision.HIGHEST)
        return out.astype(jnp.bfloat16)

    outs = lax.map(one_group, (grouped, ups))
    return outs.transpose(1, 0, 2, 3).reshape(S, H, DV)
```

```python
import math

import jax
import jax.numpy as jnp
from jax import lax
from jax.experimental import pallas as pl
from jax.experimental.pallas import tpu as pltpu
from jax.sharding import Mesh, PartitionSpec as P

DC = 512
DR = 64
NOPE = 128
DV = 128
WIDE = 640
HL = 4
TOK = 16
NH = 16
NZ = 8
SLOTS = 2048
ROWS = NH * TOK * HL
BLK = 512
NBLK = SLOTS // BLK
RC = 256
SCALE2 = (NOPE + DR) ** (-0.5) * math.log2(math.e)
LOW = -1e30
BF = jnp.bfloat16
F32 = jnp.float32
VM = pl.BlockSpec(memory_space=pltpu.VMEM)
SM = pl.BlockSpec(memory_space=pltpu.SMEM)
ANY = pl.BlockSpec(memory_space=pl.ANY)
HEAD = ("y", "x")
CTX = ("z", "core")


def dot(a, b):
    return jnp.dot(a, b, preferred_element_type=F32)


def pack_kernel(core_ref, q_ref, out_ref):
    core = core_ref[0]
    r = lax.broadcasted_iota(jnp.int32, (256, 512), 0)
    c = lax.broadcasted_iota(jnp.int32, (256, 512), 1)
    head = 8 * (r // 16) + 4 * core + r % 4
    pick = ((r // 4) % 4 == c // 128) & (head == c % 128)
    pick = jnp.where(pick, 1.0, 0.0).astype(BF)
    rot = []
    for t in range(4):
        x = jnp.concatenate([q_ref[4 * t + i] for i in range(4)], axis=1)
        y = lax.dot_general(pick, x, (((1,), (1,)), ((), ())), preferred_element_type=F32).astype(BF)
        for j in range(4):
            out_ref[:, 64 * j + 16 * t : 64 * j + 16 * t + 16, :] = y[:, 128 * j : 128 * j + 128].reshape(16, 16, 128)
        rot.append(y[:, DC:])
    for t in range(2):
        out_ref[:, 256 + 16 * t : 272 + 16 * t, :] = jnp.concatenate([rot[t], rot[t + 2]], axis=1).reshape(16, 16, 128)


def pack(core, q):
    return pl.pallas_call(
        pack_kernel,
        out_shape=jax.ShapeDtypeStruct((NH, 288, 128), BF),
        in_specs=[SM, VM],
        out_specs=VM,
        compiler_params=pltpu.CompilerParams(vmem_limit_bytes=24 * 2**20),
        cost_estimate=pl.CostEstimate(flops=10**9, bytes_accessed=4 * 10**6, transcendentals=0),
    )(core, q)


def turn_kernel(c_ref, out_ref):
    x = c_ref[...]
    out_ref[...] = jnp.concatenate([x, x[DC:]], axis=0).T


def turn(c):
    return pl.pallas_call(
        turn_kernel,
        grid=(NBLK,),
        out_shape=jax.ShapeDtypeStruct((SLOTS, WIDE), BF),
        in_specs=[pl.BlockSpec((DC + DR, BLK), lambda i: (0, i))],
        out_specs=pl.BlockSpec((BLK, WIDE), lambda i: (i, 0)),
        compiler_params=pltpu.CompilerParams(vmem_limit_bytes=24 * 2**20),
        cost_estimate=pl.CostEstimate(flops=10**9, bytes_accessed=5 * 10**6, transcendentals=0),
    )(c)


def attend_kernel(sc_ref, q_ref, w_ref, k0, k1, v0, v1, out_ref, k_scr, v_scr, qt, acc, ml, sem):
    core = sc_ref[0]
    span = sc_ref[1]
    ks, vs = (k0, k1), (v0, v1)
    bases = [sc_ref[4 + s] * SLOTS for s in range(2)]
    many = []
    for s in range(2):
        reach = jnp.clip(span + 256 - bases[s], 0, SLOTS)
        many.append((jnp.minimum(sc_ref[2 + s], reach) + BLK - 1) // BLK)

    def copies(s, i):
        lo = i * BLK
        if not isinstance(i, int):
            lo = pl.multiple_of(lo, BLK)
        return (
            pltpu.make_async_copy(ks[s].at[pl.ds(lo, BLK), :], k_scr.at[s, i], sem.at[0, s, i]),
            pltpu.make_async_copy(vs[s].at[pl.ds(0, DC), pl.ds(lo, BLK)], v_scr.at[s, i], sem.at[1, s, i]),
        )

    for s in range(2):
        for i in range(NBLK):

            @pl.when(i < many[s])
            def _():
                for c in copies(s, i):
                    c.start()

    acc[...] = jnp.zeros_like(acc)
    ml[0:1] = jnp.full((1, ROWS), LOW, F32)
    ml[1:2] = jnp.zeros((1, ROWS), F32)
    for j in range(4):
        qt[128 * j : 128 * j + 128, :] = q_ref[:, 64 * j : 64 * j + 64, :].reshape(ROWS, 128).T
    rot = q_ref[:, 256:288, :]
    lane = lax.broadcasted_iota(jnp.int32, rot.shape, 2)
    nil = jnp.zeros_like(rot)
    rot = jnp.concatenate([jnp.where(lane < 64, rot, nil), jnp.where(lane < 64, nil, rot)], axis=1)
    qt[DC:WIDE, :] = rot.reshape(ROWS, 128).T

    slot = lax.broadcasted_iota(jnp.int32, (BLK, RC), 0)
    for s in range(2):

        def block(i, _, s=s):
            for c in copies(s, i):
                c.wait()
            kb, vb = k_scr[s, i], v_scr[s, i]
            for rc in range(ROWS // RC):
                cols = slice(RC * rc, RC * rc + RC)
                token = (lax.broadcasted_iota(jnp.int32, (1, RC), 1) + RC * rc) // HL
                limit = jnp.minimum(sc_ref[2 + s], span + 1 + token - bases[s]) - i * BLK
                sco = dot(kb, qt[:, cols])
                sco = jnp.where(slot < limit, sco, LOW)
                old = ml[0:1, cols]
                new = jnp.maximum(old, jnp.max(sco, axis=0, keepdims=True))
                p = jnp.exp2((sco - new) * SCALE2)
                shrink = jnp.exp2((old - new) * SCALE2)
                ml[0:1, cols] = new
                ml[1:2, cols] = ml[1:2, cols] * shrink + jnp.sum(p, axis=0, keepdims=True)
                acc[:, cols] = acc[:, cols] * shrink + dot(vb, p.astype(BF))
            return 0

        lax.fori_loop(0, many[s], block, 0)

    for rc in range(ROWS // RC):
        cols = slice(RC * rc, RC * rc + RC)
        total = jnp.maximum(ml[1:2, cols], 1.0)
        lse = ml[0:1, cols] * SCALE2 + jnp.log2(total)
        part = (acc[:, cols] / total).astype(BF)
        up = dot(w_ref[...], part)
        which = lax.broadcasted_iota(jnp.int32, (1, RC), 1) % HL
        res = jnp.zeros((DV, RC), F32)
        for h in range(HL):
            res = jnp.where(which == h, up[DV * h : DV * h + DV], res)
        hi = lse.astype(BF)
        rest = lse - hi.astype(F32)
        mid = rest.astype(BF)
        low = (rest - mid.astype(F32)).astype(BF)
        row = lax.broadcasted_iota(jnp.int32, (16, RC), 0)
        tail = jnp.where(row == 0, hi.astype(F32), jnp.where(row == 1, mid.astype(F32), low.astype(F32)))
        res, tail = res.astype(BF), tail.astype(BF)
        for u in range(RC // 128):
            z = rc * (RC // 128) + u
            out_ref[z, 0:DV, :] = res[:, 128 * u : 128 * u + 128]
            out_ref[z, DV : DV + 16, :] = tail[:, 128 * u : 128 * u + 128]


def attend(sc, q, w, k0, k1, v0, v1):
    return pl.pallas_call(
        attend_kernel,
        out_shape=jax.ShapeDtypeStruct((NZ, DV + 16, 128), BF),
        in_specs=[SM, VM, VM, ANY, ANY, ANY, ANY],
        out_specs=VM,
        scratch_shapes=[
            pltpu.VMEM((2, NBLK, BLK, WIDE), BF),
            pltpu.VMEM((2, NBLK, DC, BLK), BF),
            pltpu.VMEM((WIDE, ROWS), BF),
            pltpu.VMEM((DC, ROWS), F32),
            pltpu.VMEM((8, ROWS), F32),
            pltpu.SemaphoreType.DMA((2, 2, NBLK)),
        ],
        compiler_params=pltpu.CompilerParams(vmem_limit_bytes=40 * 2**20),
        cost_estimate=pl.CostEstimate(flops=10**10, bytes_accessed=12 * 10**6, transcendentals=4 * 10**6),
    )(sc, q, w, k0, k1, v0, v1)


def merge_kernel(core_ref, x_ref, keep_ref, send_ref, scr):
    core = core_ref[0]
    lses = []
    for z in range(NZ):
        t = x_ref[z, DV : DV + 16, :].astype(F32)
        lses.append(t[0:1] + t[1:2] + t[2:3])
    top = lses[0]
    for z in range(1, NZ):
        top = jnp.maximum(top, lses[z])
    num = jnp.zeros((DV, 128), F32)
    den = jnp.zeros((1, 128), F32)
    for z in range(NZ):
        wz = jnp.exp2(lses[z] - top)
        den = den + wz
        num = num + wz * x_ref[z, 0:DV, :].astype(F32)
    out = (num / den).T
    scr[0] = out[:64]
    scr[1] = out[64:]
    keep_ref[...] = scr[core].astype(BF)
    send_ref[...] = scr[1 - core].astype(BF)


def merge(core, x):
    return pl.pallas_call(
        merge_kernel,
        out_shape=(jax.ShapeDtypeStruct((64, 128), BF), jax.ShapeDtypeStruct((64, 128), BF)),
        in_specs=[SM, VM],
        out_specs=(VM, VM),
        scratch_shapes=[pltpu.VMEM((2, 64, 128), F32)],
        cost_estimate=pl.CostEstimate(flops=10**6, bytes_accessed=3 * 10**5, transcendentals=1000),
    )(core, x)


def body(queries, cache, cache_len, span_start, value_up):
    core = lax.axis_index("core")
    shard = lax.axis_index(CTX)
    swap = [(0, 1), (1, 0)]
    core_a = core.reshape(1).astype(jnp.int32)
    packed = pack(core_a, queries.transpose(0, 2, 1))
    q = lax.all_to_all(packed, HEAD, split_axis=0, concat_axis=0, tiled=True)
    mine = cache.T
    other = lax.ppermute(mine, "core", swap)
    other_len = lax.ppermute(cache_len, "core", swap)
    k0, k1 = turn(mine), turn(other)
    w = lax.dynamic_slice_in_dim(value_up, HL * core, HL, 0).transpose(0, 2, 1).reshape(HL * DV, DC)
    sc = jnp.stack([core, span_start[0], cache_len[0], other_len[0], shard, shard + 1 - 2 * core, 0, 0]).astype(jnp.int32)
    part = attend(sc, q, w, k0, k1, mine, other)
    parts = lax.all_to_all(part, "z", split_axis=0, concat_axis=0, tiled=True)
    keep, send = merge(core_a, parts)
    got = lax.ppermute(send, "core", swap)
    keep, got = keep.reshape(TOK, HL, DV), got.reshape(TOK, HL, DV)
    first = jnp.where(core == 0, keep, got)
    second = jnp.where(core == 0, got, keep)
    return jnp.concatenate([first, second], axis=1)


def solution(mesh):
    fine = Mesh(mesh.devices.reshape(4, 4, 8, 2), ("y", "x", "z", "core"))
    placed = (P(HEAD, None, None), P(CTX, None), P(CTX), P(), P(HEAD, None, None))
    return jax.shard_map(body, mesh=fine, in_specs=placed, out_specs=P(CTX, HEAD, None), check_vma=False)
```

```python
import functools
import math

import jax
import jax.numpy as jnp
from jax import lax
from jax.experimental import pallas as pl
from jax.experimental.pallas import tpu as pltpu
from jax.sharding import Mesh, PartitionSpec as P

DC = 512
DR = 64
NOPE = 128
DV = 128
WIDE = 640
HL = 4
NC = 1
HC = HL // NC
TOK = 16
TG = 16 // HC
NG = TOK // TG
CR = TOK * HC
QR = CR * 9 // 2
NH = 16
NX = 16
SLOTS = 2048
ROWS = NH * CR
BLK = 1024
NBLK = SLOTS // BLK
SCALE2 = (NOPE + DR) ** (-0.5) * math.log2(math.e)
LOW = -1e30
BF = jnp.bfloat16
F32 = jnp.float32
VM = pl.BlockSpec(memory_space=pltpu.VMEM)
SM = pl.BlockSpec(memory_space=pltpu.SMEM)
ANY = pl.BlockSpec(memory_space=pl.ANY)
HEAD = ("y", "x")
CTX = ("z", "core")
BIG = 60 * 2**20


def dot(a, b):
    return jnp.dot(a, b, preferred_element_type=F32)


def iota(shape, dim):
    return lax.broadcasted_iota(jnp.int32, shape, dim)


def pack_kernel(chunk, core_ref, q_ref, out_ref, q_scr, o_scr, sem, osem):
    loads = [pltpu.make_async_copy(q_ref.at[t], q_scr.at[t], sem.at[t]) for t in range(TOK)]
    for c in loads:
        c.start()
    core = core_ref[0]
    shape = (NH * 16, TG * 128)
    r, c = iota(shape, 0), iota(shape, 1)
    head = 8 * (r // 16) + HL * core + HC * chunk + r % HC
    pick = ((r // HC) % TG == c // 128) & (head == c % 128)
    pick = jnp.where(pick, 1.0, 0.0).astype(BF)
    rot = []
    for t in range(NG):
        for i in range(TG):
            loads[TG * t + i].wait()
        x = jnp.concatenate([q_scr[TG * t + i] for i in range(TG)], axis=1)
        y = lax.dot_general(pick, x, (((1,), (1,)), ((), ())), preferred_element_type=F32).astype(BF)
        for j in range(4):
            o_scr[:, CR * j + 16 * t : CR * j + 16 * t + 16, :] = y[:, 128 * j : 128 * j + 128].reshape(NH, 16, 128)
        rot.append(y[:, DC:])
    for t in range(NG // 2):
        pair = jnp.concatenate([rot[t], rot[t + NG // 2]], axis=1)
        o_scr[:, 4 * CR + 16 * t : 4 * CR + 16 * t + 16, :] = pair.reshape(NH, 16, 128)
    stores = [pltpu.make_async_copy(o_scr.at[g], out_ref.at[g], osem.at[g]) for g in range(NH)]
    for c in stores:
        c.start()
    for c in stores:
        c.wait()


def pack(core, q, chunk):
    return pl.pallas_call(
        functools.partial(pack_kernel, chunk),
        out_shape=jax.ShapeDtypeStruct((NH, QR, 128), BF),
        in_specs=[SM, ANY],
        out_specs=ANY,
        scratch_shapes=[
            pltpu.VMEM((TOK, DC + DR, 128), BF),
            pltpu.VMEM((NH, QR, 128), BF),
            pltpu.SemaphoreType.DMA((TOK,)),
            pltpu.SemaphoreType.DMA((NH,)),
        ],
        compiler_params=pltpu.CompilerParams(vmem_limit_bytes=BIG),
        cost_estimate=pl.CostEstimate(flops=10**9, bytes_accessed=4 * 10**6, transcendentals=0),
    )(core, q)


def turn_kernel(c_ref, out_ref):
    x = c_ref[...]
    out_ref[...] = jnp.concatenate([x, x[DC:]], axis=0).T


def turn(c):
    return pl.pallas_call(
        turn_kernel,
        grid=(4,),
        out_shape=jax.ShapeDtypeStruct((SLOTS, WIDE), BF),
        in_specs=[pl.BlockSpec((DC + DR, SLOTS // 4), lambda i: (0, i))],
        out_specs=pl.BlockSpec((SLOTS // 4, WIDE), lambda i: (i, 0)),
        compiler_params=pltpu.CompilerParams(vmem_limit_bytes=BIG),
        cost_estimate=pl.CostEstimate(flops=10**9, bytes_accessed=5 * 10**6, transcendentals=0),
    )(c)


def attend_kernel(sc_ref, q_ref, w_ref, k0, k1, v0, v1, out_ref, q_scr, w_scr, k_scr, v_scr, qt, sco, acc, ml, sem):
    span = sc_ref[1]
    ks, vs = (k0, k1), (v0, v1)
    qcopy = pltpu.make_async_copy(q_ref, q_scr, sem.at[2, 0])
    wcopy = pltpu.make_async_copy(w_ref, w_scr, sem.at[2, 1])
    kcopy, vcopy = [], []
    for b in range(2 * NBLK):
        at = pl.ds(b % NBLK * BLK, BLK)
        kcopy.append(pltpu.make_async_copy(ks[b // NBLK].at[at, :], k_scr.at[b], sem.at[0, b]))
        vcopy.append(pltpu.make_async_copy(vs[b // NBLK].at[pl.ds(0, DC), at], v_scr.at[b], sem.at[1, b]))
    qcopy.start()
    for c in kcopy:
        c.start()
    for c in vcopy:
        c.start()
    wcopy.start()

    qcopy.wait()
    for j in range(4):
        qt[128 * j : 128 * j + 128, :] = q_scr[:, CR * j : CR * j + CR, :].reshape(ROWS, 128).T
    rot = q_scr[:, 4 * CR :, :]
    lane = iota(rot.shape, 2)
    nil = jnp.zeros_like(rot)
    rot = jnp.concatenate([jnp.where(lane < 64, rot, nil), jnp.where(lane < 64, nil, rot)], axis=1)
    qt[DC:WIDE, :] = rot.reshape(ROWS, 128).T

    token = iota((1, ROWS), 1) // HC
    slot = iota((BLK, ROWS), 0)
    top = jnp.full((1, ROWS), LOW, F32)
    for b in range(2 * NBLK):
        s = b // NBLK
        limit = jnp.minimum(sc_ref[2 + s], span + 1 + token - sc_ref[4 + s] * SLOTS) - b % NBLK * BLK
        kcopy[b].wait()
        x = jnp.where(slot < limit, dot(k_scr[b], qt[...]), LOW)
        sco[b] = x
        top = jnp.maximum(top, jnp.max(x, axis=0, keepdims=True))
    ml[0:1] = top

    total = jnp.zeros((1, ROWS), F32)
    for b in range(2 * NBLK):
        vcopy[b].wait()
        p = jnp.exp2((sco[b] - ml[0:1]) * SCALE2)
        total = total + jnp.sum(p, axis=0, keepdims=True)
        up = dot(v_scr[b], p.astype(BF))
        acc[...] = up if b == 0 else acc[...] + up

    wcopy.wait()
    total = jnp.maximum(total, 1.0)
    lse = ml[0:1] * SCALE2 + jnp.log2(total)
    up = dot(w_scr[...], (acc[...] / total).astype(BF))
    which = iota((1, ROWS), 1) % HC
    res = up[0:DV]
    for h in range(1, HC):
        res = jnp.where(which == h, up[DV * h : DV * h + DV], res)
    out_ref[:, 0:CR, :] = res.T.astype(BF).reshape(NH, CR, DV)
    hi = lse.astype(BF).astype(F32)
    mid = (lse - hi).astype(BF).astype(F32)
    low = lse - hi - mid
    row = iota((16, ROWS), 0)
    tail = jnp.where(row == 0, hi, jnp.where(row == 1, mid, low)).astype(BF)
    for a in range(NX):
        line = a * CR // 128 * 128
        out_ref[a, CR : CR + 16, :] = tail[:, line : line + 128]


def attend(sc, q, w, k0, k1, v0, v1):
    return pl.pallas_call(
        attend_kernel,
        out_shape=jax.ShapeDtypeStruct((NX, CR + 16, 128), BF),
        in_specs=[SM, ANY, ANY, ANY, ANY, ANY, ANY],
        out_specs=VM,
        scratch_shapes=[
            pltpu.VMEM((NH, QR, 128), BF),
            pltpu.VMEM((HC * DV, DC), BF),
            pltpu.VMEM((2 * NBLK, BLK, WIDE), BF),
            pltpu.VMEM((2 * NBLK, DC, BLK), BF),
            pltpu.VMEM((WIDE, ROWS), BF),
            pltpu.VMEM((2 * NBLK, BLK, ROWS), F32),
            pltpu.VMEM((DC, ROWS), F32),
            pltpu.VMEM((8, ROWS), F32),
            pltpu.SemaphoreType.DMA((3, max(2 * NBLK, 2))),
        ],
        compiler_params=pltpu.CompilerParams(vmem_limit_bytes=BIG),
        cost_estimate=pl.CostEstimate(flops=10**10, bytes_accessed=12 * 10**6, transcendentals=4 * 10**6),
    )(sc, q, w, k0, k1, v0, v1)


def merge_kernel(sc_ref, *refs):
    xs, out_ref, scr = refs[:NC], refs[NC], refs[NC + 1]
    lines = []
    for x in xs:
        for k in range(2):
            lse = []
            for z in range(NX // 2):
                t = x[2 * z + k, CR : CR + 16, :].astype(F32)
                lse.append(t[0:1] + t[1:2] + t[2:3])
            lse = jnp.concatenate(lse, axis=0)
            wz = jnp.exp2(lse - jnp.max(lse, axis=0, keepdims=True))
            lines.append(wz / jnp.sum(wz, axis=0, keepdims=True))
    lines.append(jnp.zeros((128 - 16 * NC, 128), F32))
    scr[...] = jnp.concatenate(lines, axis=0).T
    off = sc_ref[6] % (128 // CR) * CR
    wt = scr[pl.ds(pl.multiple_of(off, CR), CR), :]
    merged = []
    for c, x in enumerate(xs):
        for k in range(2):
            num = jnp.zeros((CR, DV), F32)
            for z in range(NX // 2):
                at = c * NX + k * (NX // 2) + z
                num = num + wt[:, at : at + 1] * x[2 * z + k, 0:CR, :].astype(F32)
            merged.append(num.astype(BF))
    merged = jnp.concatenate(merged, axis=0)
    r, c = iota((128, 128), 0), iota((128, 128), 1)
    head = HL * (c // CR % 2) + HC * (c // (2 * CR)) + c % HC
    pick = (r // 8 == c % CR // HC) & (r % 8 == head)
    out_ref[...] = dot(jnp.where(pick, 1.0, 0.0).astype(BF), merged).astype(BF)


def merge(sc, xs):
    return pl.pallas_call(
        merge_kernel,
        out_shape=jax.ShapeDtypeStruct((TOK * 2 * HL, DV), BF),
        in_specs=[SM] + [VM] * NC,
        out_specs=VM,
        scratch_shapes=[pltpu.VMEM((128, 128), F32)],
        cost_estimate=pl.CostEstimate(flops=10**6, bytes_accessed=3 * 10**5, transcendentals=1000),
    )(sc, *xs)


def body(queries, cache, cache_len, span_start, value_up):
    core = lax.axis_index("core")
    shard = lax.axis_index(CTX)
    swap = [(0, 1), (1, 0)]
    core_a = core.reshape(1).astype(jnp.int32)
    turned = queries.transpose(0, 2, 1)
    q = [
        lax.all_to_all(pack(core_a, turned, c), HEAD, split_axis=0, concat_axis=0, tiled=True) for c in range(NC)
    ]
    mine = cache.T
    other = lax.ppermute(mine, "core", swap)
    other_len = lax.ppermute(cache_len, "core", swap)
    k0, k1 = turn(mine), turn(other)
    sc = jnp.stack([core, span_start[0], cache_len[0], other_len[0], shard, shard + 1 - 2 * core, shard, 0]).astype(jnp.int32)
    parts = []
    for c in range(NC):
        w = lax.dynamic_slice_in_dim(value_up, HL * core + HC * c, HC, 0).transpose(0, 2, 1).reshape(HC * DV, DC)
        part = attend(sc, q[c], w, k0, k1, mine, other)
        parts.append(lax.all_to_all(part, CTX, split_axis=0, concat_axis=0, tiled=True))
    return merge(sc, parts).reshape(TOK, 2 * HL, DV)


def solution(mesh):
    fine = Mesh(mesh.devices.reshape(4, 4, 8, 2), ("y", "x", "z", "core"))
    placed = (P(HEAD, None, None), P(CTX, None), P(CTX), P(), P(HEAD, None, None))
    return jax.shard_map(body, mesh=fine, in_specs=placed, out_specs=P(CTX, HEAD, None), check_vma=False)
```

```python
import math

import jax
import jax.numpy as jnp
from jax import lax
from jax.experimental import pallas as pl
from jax.experimental.pallas import tpu as pltpu
from jax.sharding import Mesh, PartitionSpec as P

DC = 512
DR = 64
NOPE = 128
DV = 128
WIDE = DC + DR
HL = 4
TOK = 16
TG = 16 // HL
CR = TOK * HL
QR = CR * 9 // 2
NH = 16
NX = 16
SLOTS = 2048
ROWS = NH * CR
BLK = 1024
NBLK = SLOTS // BLK
SCALE2 = (NOPE + DR) ** (-0.5) * math.log2(math.e)
LOW = -1e30
BF = jnp.bfloat16
F32 = jnp.float32
VM = pl.BlockSpec(memory_space=pltpu.VMEM)
SM = pl.BlockSpec(memory_space=pltpu.SMEM)
HB = pl.BlockSpec(memory_space=pltpu.HBM)
GRANT = 119 * 2**19
HEAD = ("y", "x")
CTX = ("z", "core")


def dot(a, b):
    return jnp.dot(a, b, preferred_element_type=F32)


def iota(shape, dim):
    return lax.broadcasted_iota(jnp.int32, shape, dim)


def pack_kernel(q_ref, out_ref):
    shape = (NH * 16, TG * 128)
    r, c = iota(shape, 0), iota(shape, 1)
    head = 8 * (r // 16) + HL * lax.axis_index("core") + r % HL
    pick = ((r // HL) % TG == c // 128) & (head == c % 128)
    pick = jnp.where(pick, 1.0, 0.0).astype(BF)
    rot = []
    for t in range(2):
        x = jnp.concatenate([q_ref[TG * t + i] for i in range(TG)], axis=1)
        y = lax.dot_general(pick, x, (((1,), (1,)), ((), ())), preferred_element_type=F32).astype(BF)
        for j in range(4):
            out_ref[:, 32 * j + 16 * t : 32 * j + 16 * t + 16, :] = y[:, 128 * j : 128 * j + 128].reshape(NH, 16, 128)
        rot.append(y[:, DC:])
    out_ref[:, 128:144, :] = jnp.concatenate(rot, axis=1).reshape(NH, 16, 128)


def pack(q):
    return pl.pallas_call(
        pack_kernel,
        grid=(2,),
        out_shape=jax.ShapeDtypeStruct((NH, QR, 128), BF),
        in_specs=[pl.BlockSpec((2 * TG, WIDE, 128), lambda u: (u, 0, 0))],
        out_specs=pl.BlockSpec((NH, QR // 2, 128), lambda u: (0, u, 0)),
        compiler_params=pltpu.CompilerParams(vmem_limit_bytes=GRANT),
        cost_estimate=pl.CostEstimate(flops=10**9, bytes_accessed=4 * 10**6, transcendentals=0),
    )(q)


def attend_kernel(len0, len1, span_ref, q_ref, w_ref, c0, c1, out_ref, w_scr, c_scr, qr, sco, acc, ml, sem, wsem):
    core, span = lax.axis_index("core"), span_ref[0]
    shard = 2 * lax.axis_index("z") + core
    wcopy = pltpu.make_async_copy(w_ref.at[pl.ds(HL * core, HL)], w_scr, wsem)
    loads = []
    for b in range(2 * NBLK):
        src = (c0, c1)[b // NBLK].at[:, pl.ds(b % NBLK * BLK, BLK)]
        loads.append(pltpu.make_async_copy(src, c_scr.at[b], sem.at[b]))
    loads[0].start()

    for u in range(2):
        for j in range(4):
            line = 144 * u + 32 * j
            qr[:, 32 * u : 32 * u + 32, 128 * j : 128 * j + 128] = q_ref[:, line : line + 32, :]
        rot = q_ref[:, 144 * u + 128 : 144 * u + 144, :]
        qr[:, 32 * u : 32 * u + 16, DC:WIDE] = rot[:, :, 0:DR]
        qr[:, 32 * u + 16 : 32 * u + 32, DC:WIDE] = rot[:, :, DR:]

    token = iota((1, ROWS), 1) // HL
    slot = iota((BLK, ROWS), 0)
    ml[0:1] = jnp.full((1, ROWS), LOW, F32)
    ml[1:2] = jnp.zeros((1, ROWS), F32)
    acc[...] = jnp.zeros_like(acc)

    def score(b, _):
        pltpu.make_async_copy(c0.at[:, pl.ds(0, BLK)], c_scr.at[b], sem.at[b]).wait()

        @pl.when(b == 0)
        def _():
            for c in loads[1:]:
                c.start()
            wcopy.start()

        s = b // NBLK
        filled = jnp.where(s == 0, len0[0], len1[0])
        first = jnp.where(s == 0, shard, shard + 1 - 2 * core) * SLOTS
        limit = jnp.minimum(filled, span + 1 + token - first) - b % NBLK * BLK
        x = lax.dot_general(c_scr[b], qr[...].reshape(ROWS, WIDE), (((0,), (1,)), ((), ())), preferred_element_type=F32)
        x = jnp.where(slot < limit, x, LOW)
        sco[b] = x
        ml[0:1] = jnp.maximum(ml[0:1], jnp.max(x, axis=0, keepdims=True))
        return 0

    def weigh(b, _):
        p = jnp.exp2((sco[b] - ml[0:1]) * SCALE2)
        ml[1:2] = ml[1:2] + jnp.sum(p, axis=0, keepdims=True)
        acc[...] += dot(c_scr[b, 0:DC], p.astype(BF))
        return 0

    lax.fori_loop(0, 2 * NBLK, score, 0, unroll=2)
    lax.fori_loop(0, 2 * NBLK, weigh, 0, unroll=2)

    wcopy.wait()
    total = jnp.maximum(ml[1:2], 1.0)
    lse = ml[0:1] * SCALE2 + jnp.log2(total)
    part = (acc[...] * (1.0 / total)).astype(BF)
    which = iota((1, ROWS), 1) % HL
    res = jnp.zeros((DV, ROWS), F32)
    for h in range(HL):
        up = lax.dot_general(w_scr[h], part, (((0,), (0,)), ((), ())), preferred_element_type=F32)
        res = jnp.where(which == h, up, res)
    out_ref[:, 0:CR, :] = res.T.astype(BF).reshape(NH, CR, DV)
    hi = lse.astype(BF).astype(F32)
    mid = (lse - hi).astype(BF).astype(F32)
    low = lse - hi - mid
    row = iota((16, ROWS), 0)
    tail = jnp.where(row == 0, hi, jnp.where(row == 1, mid, low)).astype(BF)
    for a in range(NX):
        line = a * CR // 128 * 128
        out_ref[a, CR : CR + 16, :] = tail[:, line : line + 128]


def attend(len0, len1, span, q, w, c0, c1):
    return pl.pallas_call(
        attend_kernel,
        out_shape=jax.ShapeDtypeStruct((NX, CR + 16, 128), BF),
        in_specs=[SM, SM, SM, VM, HB, HB, HB],
        out_specs=VM,
        scratch_shapes=[
            pltpu.VMEM((HL, DC, DV), BF),
            pltpu.VMEM((2 * NBLK, WIDE, BLK), BF),
            pltpu.VMEM((NH, CR, WIDE), BF),
            pltpu.VMEM((2 * NBLK, BLK, ROWS), F32),
            pltpu.VMEM((DC, ROWS), F32),
            pltpu.VMEM((8, ROWS), F32),
            pltpu.SemaphoreType.DMA((2 * NBLK,)),
            pltpu.SemaphoreType.DMA,
        ],
        compiler_params=pltpu.CompilerParams(vmem_limit_bytes=44 * 2**20),
        cost_estimate=pl.CostEstimate(flops=10**10, bytes_accessed=6 * 10**6, transcendentals=4 * 10**6),
    )(len0, len1, span, q, w, c0, c1)


def merge_kernel(x_ref, out_ref, scr):
    lines = []
    for k in range(2):
        lse = []
        for z in range(NX // 2):
            t = x_ref[2 * z + k, CR : CR + 16, :].astype(F32)
            lse.append(t[0:1] + t[1:2] + t[2:3])
        lse = jnp.concatenate(lse, axis=0)
        wz = jnp.exp2(lse - jnp.max(lse, axis=0, keepdims=True))
        lines.append(wz / jnp.sum(wz, axis=0, keepdims=True))
    lines.append(jnp.zeros((128 - NX, 128), F32))
    scr[...] = jnp.concatenate(lines, axis=0).T
    off = lax.axis_index("core") * CR
    wt = scr[pl.ds(pl.multiple_of(off, CR), CR), :]
    merged = []
    for k in range(2):
        num = jnp.zeros((CR, DV), F32)
        for z in range(NX // 2):
            at = k * (NX // 2) + z
            num = num + wt[:, at : at + 1] * x_ref[2 * z + k, 0:CR, :].astype(F32)
        merged.append(num.astype(BF))
    merged = jnp.concatenate(merged, axis=0)
    r, c = iota((128, 128), 0), iota((128, 128), 1)
    pick = (r // 8 == c % CR // HL) & (r % 8 == HL * (c // CR) + c % HL)
    out_ref[...] = dot(jnp.where(pick, 1.0, 0.0).astype(BF), merged).astype(BF)


def merge(x):
    return pl.pallas_call(
        merge_kernel,
        out_shape=jax.ShapeDtypeStruct((TOK * 2 * HL, DV), BF),
        in_specs=[VM],
        out_specs=VM,
        scratch_shapes=[pltpu.VMEM((128, 128), F32)],
        compiler_params=pltpu.CompilerParams(vmem_limit_bytes=8 * 2**20),
        cost_estimate=pl.CostEstimate(flops=10**6, bytes_accessed=3 * 10**5, transcendentals=1000),
    )(x)


def body(queries, cache, cache_len, span_start, value_up):
    swap = [(0, 1), (1, 0)]
    mine = cache.T
    other = lax.ppermute(mine, "core", swap)
    other_len = lax.ppermute(cache_len, "core", swap)
    q = lax.all_to_all(pack(queries.transpose(0, 2, 1)), HEAD, split_axis=0, concat_axis=0, tiled=True)
    up = pltpu.with_memory_space_constraint(value_up, pltpu.HBM)
    part = attend(cache_len, other_len, span_start, q, up, mine, other)
    part = lax.all_to_all(part, CTX, split_axis=0, concat_axis=0, tiled=True)
    return merge(part).reshape(TOK, 2 * HL, DV)


def solution(mesh):
    fine = Mesh(mesh.devices.reshape(4, 4, 8, 2), ("y", "x", "z", "core"))
    placed = (P(HEAD, None, None), P(CTX, None), P(CTX), P(), P(HEAD, None, None))
    return jax.shard_map(body, mesh=fine, in_specs=placed, out_specs=P(CTX, HEAD, None), check_vma=False)
```

```python
import math

import jax
import jax.numpy as jnp
from jax import lax
from jax.experimental import pallas as pl
from jax.experimental.pallas import tpu as pltpu
from jax.sharding import Mesh, PartitionSpec as P

DC = 512
DR = 64
NOPE = 128
DV = 128
WIDE = DC + DR
HL = 4
TOK = 16
TG = 16 // HL
CR = TOK * HL
QR = CR * 9 // 2
NH = 16
NX = 16
SLOTS = 2048
ROWS = NH * CR
BLK = 1024
NBLK = SLOTS // BLK
SCALE2 = (NOPE + DR) ** (-0.5) * math.log2(math.e)
LOW = -1e30
BF = jnp.bfloat16
F32 = jnp.float32
VM = pl.BlockSpec(memory_space=pltpu.VMEM)
SM = pl.BlockSpec(memory_space=pltpu.SMEM)
HB = pl.BlockSpec(memory_space=pltpu.HBM)
GRANT = 119 * 2**19
HEAD = ("y", "x")
CTX = ("z", "core")


def dot(a, b):
    return jnp.dot(a, b, preferred_element_type=F32)


def iota(shape, dim):
    return lax.broadcasted_iota(jnp.int32, shape, dim)


def pack_kernel(q_ref, out_ref):
    shape = (NH * 16, TG * 128)
    r, c = iota(shape, 0), iota(shape, 1)
    head = 8 * (r // 16) + HL * lax.axis_index("core") + r % HL
    pick = ((r // HL) % TG == c // 128) & (head == c % 128)
    pick = jnp.where(pick, 1.0, 0.0).astype(BF)
    rot = []
    for t in range(2):
        x = jnp.concatenate([q_ref[TG * t + i] for i in range(TG)], axis=1)
        y = lax.dot_general(pick, x, (((1,), (1,)), ((), ())), preferred_element_type=F32).astype(BF)
        for j in range(4):
            out_ref[:, 32 * j + 16 * t : 32 * j + 16 * t + 16, :] = y[:, 128 * j : 128 * j + 128].reshape(NH, 16, 128)
        rot.append(y[:, DC:])
    out_ref[:, 128:144, :] = jnp.concatenate(rot, axis=1).reshape(NH, 16, 128)


def pack(q):
    return pl.pallas_call(
        pack_kernel,
        grid=(2,),
        out_shape=jax.ShapeDtypeStruct((NH, QR, 128), BF),
        in_specs=[pl.BlockSpec((2 * TG, WIDE, 128), lambda u: (u, 0, 0))],
        out_specs=pl.BlockSpec((NH, QR // 2, 128), lambda u: (0, u, 0)),
        compiler_params=pltpu.CompilerParams(vmem_limit_bytes=GRANT),
        cost_estimate=pl.CostEstimate(flops=10**9, bytes_accessed=4 * 10**6, transcendentals=0),
    )(q)


def fold_kernel(w_ref, c0, c1, out_ref):
    core = lax.axis_index("core")
    w = jnp.concatenate([w_ref[HL * core + h] for h in range(HL)], axis=1)
    for b in range(2 * NBLK):
        c = (c0, c1)[b // NBLK][0:DC, b % NBLK * BLK : b % NBLK * BLK + BLK]
        out_ref[b] = lax.dot_general(w, c, (((0,), (0,)), ((), ())), preferred_element_type=F32).astype(BF)


def fold(w, c0, c1):
    return pl.pallas_call(
        fold_kernel,
        out_shape=jax.ShapeDtypeStruct((2 * NBLK, HL * DV, BLK), BF),
        in_specs=[VM, VM, VM],
        out_specs=VM,
        compiler_params=pltpu.CompilerParams(vmem_limit_bytes=44 * 2**20),
        cost_estimate=pl.CostEstimate(flops=2 * 10**9, bytes_accessed=10**7, transcendentals=0),
    )(w, c0, c1)


def attend_kernel(len0, len1, span_ref, q_ref, u_ref, c0, c1, out_ref, u_scr, c_scr, qr, sco, acc, ml, sem, usem):
    core, span = lax.axis_index("core"), span_ref[0]
    shard = 2 * lax.axis_index("z") + core
    loads = []
    for b in range(2 * NBLK):
        src = (c0, c1)[b // NBLK].at[:, pl.ds(b % NBLK * BLK, BLK)]
        loads.append(pltpu.make_async_copy(src, c_scr.at[b], sem.at[b]))
    loads[0].start()

    r, c = iota((256, 256), 0), iota((256, 256), 1)
    pick = (r // 64 == c % HL) & (r // 16 % 4 == c // 64) & (r % 16 == c % 64 // HL)
    pick = jnp.where(pick, 1.0, 0.0).astype(BF)
    for g in range(NH // 4):
        x = q_ref[4 * g : 4 * g + 4]
        parts = [
            jnp.concatenate([x[:, 32 * j : 32 * j + 32], x[:, 144 + 32 * j : 176 + 32 * j]], axis=1).reshape(256, 128)
            for j in range(4)
        ]
        rot = [x[:, 144 * u + 128 : 144 * u + 144, DR * v : DR * v + DR] for u in range(2) for v in range(2)]
        parts.append(jnp.concatenate(rot, axis=1).reshape(256, DR))
        for j, part in enumerate(parts):
            y = dot(pick, part).astype(BF)
            for h in range(HL):
                qr[256 * h + 64 * g : 256 * h + 64 * g + 64, 128 * j : 128 * j + y.shape[1]] = y[64 * h : 64 * h + 64]

    token = iota((1, ROWS), 1) % 256
    slot = iota((BLK, ROWS), 0)
    ml[0:1] = jnp.full((1, ROWS), LOW, F32)
    ml[1:2] = jnp.zeros((1, ROWS), F32)
    acc[...] = jnp.zeros_like(acc)

    def score(b, _):
        pltpu.make_async_copy(c0.at[:, pl.ds(0, BLK)], c_scr.at[b], sem.at[b]).wait()

        @pl.when(b == 0)
        def _():
            for c in loads[1:]:
                c.start()
            pltpu.make_async_copy(u_ref, u_scr, usem).start()

        s = b // NBLK
        filled = jnp.where(s == 0, len0[0], len1[0])
        first = jnp.where(s == 0, shard, shard + 1 - 2 * core) * SLOTS
        limit = jnp.minimum(filled, span + 1 + token - first) - b % NBLK * BLK
        x = lax.dot_general(c_scr[b], qr[...], (((0,), (1,)), ((), ())), preferred_element_type=F32)
        x = jnp.where(slot < limit, x, LOW)
        sco[b] = x
        ml[0:1] = jnp.maximum(ml[0:1], jnp.max(x, axis=0, keepdims=True))
        return 0

    def weigh(b, _):
        p = jnp.exp2((sco[b] - ml[0:1]) * SCALE2)
        ml[1:2] = ml[1:2] + jnp.sum(p, axis=0, keepdims=True)
        p = p.astype(BF)
        for h in range(HL):
            acc[:, 256 * h : 256 * h + 256] += dot(u_scr[b, DV * h : DV * h + DV], p[:, 256 * h : 256 * h + 256])
        return 0

    lax.fori_loop(0, 2 * NBLK, score, 0, unroll=2)
    pltpu.make_async_copy(u_ref, u_scr, usem).wait()
    lax.fori_loop(0, 2 * NBLK, weigh, 0, unroll=2)

    total = jnp.maximum(ml[1:2], 1.0)
    lse = ml[0:1] * SCALE2 + jnp.log2(total)
    res = (acc[...] * (1.0 / total)).T.astype(BF)
    for h in range(HL):
        out_ref[:, 16 * h : 16 * h + 16, :] = res[256 * h : 256 * h + 256].reshape(NX, 16, DV)
    hi = lse.astype(BF).astype(F32)
    mid = (lse - hi).astype(BF).astype(F32)
    low = lse - hi - mid
    for line in range(2):
        tail = [x[:, 256 * h + 128 * line : 256 * h + 128 * line + 128] for x in (hi, mid, low) for h in range(HL)]
        tail = jnp.concatenate(tail + tail[:4], axis=0).astype(BF)
        for a in range(8):
            out_ref[8 * line + a, CR : CR + 16, :] = tail


def attend(len0, len1, span, q, u, c0, c1):
    return pl.pallas_call(
        attend_kernel,
        out_shape=jax.ShapeDtypeStruct((NX, CR + 16, 128), BF),
        in_specs=[SM, SM, SM, VM, HB, HB, HB],
        out_specs=VM,
        scratch_shapes=[
            pltpu.VMEM((2 * NBLK, HL * DV, BLK), BF),
            pltpu.VMEM((2 * NBLK, WIDE, BLK), BF),
            pltpu.VMEM((ROWS, WIDE), BF),
            pltpu.VMEM((2 * NBLK, BLK, ROWS), F32),
            pltpu.VMEM((DV, ROWS), F32),
            pltpu.VMEM((8, ROWS), F32),
            pltpu.SemaphoreType.DMA((2 * NBLK,)),
            pltpu.SemaphoreType.DMA,
        ],
        compiler_params=pltpu.CompilerParams(vmem_limit_bytes=44 * 2**20),
        cost_estimate=pl.CostEstimate(flops=10**10, bytes_accessed=6 * 10**6, transcendentals=4 * 10**6),
    )(len0, len1, span, q, u, c0, c1)


def merge_kernel(x_ref, out_ref, scr):
    lines = []
    for k in range(2):
        lse = []
        for z in range(NX // 2):
            t = x_ref[2 * z + k, CR : CR + 16, :].astype(F32)
            lse.append(t[0:4] + t[4:8] + t[8:12])
        top = lse[0]
        for x in lse[1:]:
            top = jnp.maximum(top, x)
        wz = [jnp.exp2(x - top) for x in lse]
        scale = 1.0 / sum(wz)
        lines += [x * scale for x in wz]
    lines.append(jnp.zeros((128 - NX * HL, 128), F32))
    scr[...] = jnp.concatenate(lines, axis=0).T
    off = (2 * lax.axis_index("z") + lax.axis_index("core")) % 8 * TOK
    wt = scr[pl.ds(pl.multiple_of(off, TOK), TOK), :]
    merged = []
    for k in range(2):
        for h in range(HL):
            num = jnp.zeros((TOK, DV), F32)
            for z in range(NX // 2):
                at = (k * (NX // 2) + z) * HL + h
                num = num + wt[:, at : at + 1] * x_ref[2 * z + k, 16 * h : 16 * h + 16, :].astype(F32)
            merged.append(num.astype(BF))
    merged = jnp.concatenate(merged, axis=0)
    r, c = iota((128, 128), 0), iota((128, 128), 1)
    pick = (r // 8 == c % TOK) & (r % 8 == c // TOK)
    out_ref[...] = dot(jnp.where(pick, 1.0, 0.0).astype(BF), merged).astype(BF)


def merge(x):
    return pl.pallas_call(
        merge_kernel,
        out_shape=jax.ShapeDtypeStruct((TOK * 2 * HL, DV), BF),
        in_specs=[VM],
        out_specs=VM,
        scratch_shapes=[pltpu.VMEM((128, 128), F32)],
        compiler_params=pltpu.CompilerParams(vmem_limit_bytes=8 * 2**20),
        cost_estimate=pl.CostEstimate(flops=10**6, bytes_accessed=3 * 10**5, transcendentals=1000),
    )(x)


def body(queries, cache, cache_len, span_start, value_up):
    swap = [(0, 1), (1, 0)]
    mine = cache.T
    other = lax.ppermute(mine, "core", swap)
    other_len = lax.ppermute(cache_len, "core", swap)
    q = lax.all_to_all(pack(queries.transpose(0, 2, 1)), HEAD, split_axis=0, concat_axis=0, tiled=True)
    folded = pltpu.with_memory_space_constraint(fold(value_up, mine, other), pltpu.HBM)
    part = attend(cache_len, other_len, span_start, q, folded, mine, other)
    part = lax.all_to_all(part, CTX, split_axis=0, concat_axis=0, tiled=True)
    return merge(part).reshape(TOK, 2 * HL, DV)


def solution(mesh):
    fine = Mesh(mesh.devices.reshape(4, 4, 8, 2), ("y", "x", "z", "core"))
    placed = (P(HEAD, None, None), P(CTX, None), P(CTX), P(), P(HEAD, None, None))
    return jax.shard_map(body, mesh=fine, in_specs=placed, out_specs=P(CTX, HEAD, None), check_vma=False)
```

```python
import math

import jax
import jax.numpy as jnp
from jax import lax
from jax.experimental import pallas as pl
from jax.experimental.pallas import tpu as pltpu
from jax.sharding import Mesh, PartitionSpec as P

DC = 512
DR = 64
NOPE = 128
DV = 128
WIDE = DC + DR
HL = 4
TOK = 16
TG = 16 // HL
CR = TOK * HL
QR = CR * 9 // 2
NH = 16
NX = 16
SLOTS = 2048
ROWS = NH * CR
BLK = 1024
NBLK = SLOTS // BLK
SCALE2 = (NOPE + DR) ** (-0.5) * math.log2(math.e)
LOW = -1e30
BF = jnp.bfloat16
F32 = jnp.float32
VM = pl.BlockSpec(memory_space=pltpu.VMEM)
SM = pl.BlockSpec(memory_space=pltpu.SMEM)
HB = pl.BlockSpec(memory_space=pltpu.HBM)
GRANT = 119 * 2**19
HEAD = ("y", "x")
CTX = ("z", "core")


def dot(a, b):
    return jnp.dot(a, b, preferred_element_type=F32)


def iota(shape, dim):
    return lax.broadcasted_iota(jnp.int32, shape, dim)


def pack_kernel(q_ref, out_ref):
    shape = (NH * 16, TG * 128)
    r, c = iota(shape, 0), iota(shape, 1)
    head = 8 * (r // 16) + HL * lax.axis_index("core") + r % HL
    pick = ((r // HL) % TG == c // 128) & (head == c % 128)
    pick = jnp.where(pick, 1.0, 0.0).astype(BF)
    rot = []
    for t in range(2):
        x = jnp.concatenate([q_ref[TG * t + i] for i in range(TG)], axis=1)
        y = lax.dot_general(pick, x, (((1,), (1,)), ((), ())), preferred_element_type=F32).astype(BF)
        for j in range(4):
            out_ref[:, 32 * j + 16 * t : 32 * j + 16 * t + 16, :] = y[:, 128 * j : 128 * j + 128].reshape(NH, 16, 128)
        rot.append(y[:, DC:])
    out_ref[:, 128:144, :] = jnp.concatenate(rot, axis=1).reshape(NH, 16, 128)


def pack(q):
    return pl.pallas_call(
        pack_kernel,
        grid=(2,),
        out_shape=jax.ShapeDtypeStruct((NH, QR, 128), BF),
        in_specs=[pl.BlockSpec((2 * TG, WIDE, 128), lambda u: (u, 0, 0))],
        out_specs=pl.BlockSpec((NH, QR // 2, 128), lambda u: (0, u, 0)),
        compiler_params=pltpu.CompilerParams(vmem_limit_bytes=GRANT),
        cost_estimate=pl.CostEstimate(flops=10**9, bytes_accessed=4 * 10**6, transcendentals=0),
    )(q)


def fold_kernel(w_ref, c0, c1, out_ref):
    core = lax.axis_index("core")
    w = jnp.concatenate([w_ref[HL * core + h] for h in range(HL)], axis=1)
    for b in range(2 * NBLK):
        c = (c0, c1)[b // NBLK][0:DC, b % NBLK * BLK : b % NBLK * BLK + BLK]
        out_ref[b] = lax.dot_general(w, c, (((0,), (0,)), ((), ())), preferred_element_type=F32).astype(BF)


def fold(w, c0, c1):
    return pl.pallas_call(
        fold_kernel,
        out_shape=jax.ShapeDtypeStruct((2 * NBLK, HL * DV, BLK), BF),
        in_specs=[VM, VM, VM],
        out_specs=VM,
        compiler_params=pltpu.CompilerParams(vmem_limit_bytes=44 * 2**20),
        cost_estimate=pl.CostEstimate(flops=2 * 10**9, bytes_accessed=10**7, transcendentals=0),
    )(w, c0, c1)


def attend_kernel(len0, len1, span_ref, q_ref, u_ref, c0, c1, out_ref, u_scr, c_scr, qr, sco, acc, ml, sem, usem):
    core, span = lax.axis_index("core"), span_ref[0]
    shard = 2 * lax.axis_index("z") + core
    loads = []
    for b in range(2 * NBLK):
        src = (c0, c1)[b // NBLK].at[:, pl.ds(b % NBLK * BLK, BLK)]
        loads.append(pltpu.make_async_copy(src, c_scr.at[b], sem.at[b]))
    loads[0].start()

    r, c = iota((256, 256), 0), iota((256, 256), 1)
    pick = (r // 64 == c % HL) & (r // 16 % 4 == c // 64) & (r % 16 == c % 64 // HL)
    pick = jnp.where(pick, 1.0, 0.0).astype(BF)
    for g in range(NH // 4):
        x = q_ref[4 * g : 4 * g + 4]
        parts = [
            jnp.concatenate([x[:, 32 * j : 32 * j + 32], x[:, 144 + 32 * j : 176 + 32 * j]], axis=1).reshape(256, 128)
            for j in range(4)
        ]
        rot = [x[:, 144 * u + 128 : 144 * u + 144, DR * v : DR * v + DR] for u in range(2) for v in range(2)]
        parts.append(jnp.concatenate(rot, axis=1).reshape(256, DR))
        y = dot(pick, jnp.concatenate(parts, axis=1)).astype(BF)
        for h in range(HL):
            qr[256 * h + 64 * g : 256 * h + 64 * g + 64, :] = y[64 * h : 64 * h + 64]

    token = iota((1, ROWS), 1) % 256
    slot = iota((BLK, ROWS), 0)
    ml[0:1] = jnp.full((1, ROWS), LOW, F32)
    ml[1:2] = jnp.zeros((1, ROWS), F32)
    acc[...] = jnp.zeros_like(acc)

    def score(b, _):
        pltpu.make_async_copy(c0.at[:, pl.ds(0, BLK)], c_scr.at[b], sem.at[b]).wait()

        @pl.when(b == 0)
        def _():
            for c in loads[1:]:
                c.start()
            pltpu.make_async_copy(u_ref, u_scr, usem).start()

        s = b // NBLK
        filled = jnp.where(s == 0, len0[0], len1[0])
        first = jnp.where(s == 0, shard, shard + 1 - 2 * core) * SLOTS
        limit = jnp.minimum(filled, span + 1 + token - first) - b % NBLK * BLK
        x = lax.dot_general(c_scr[b], qr[...], (((0,), (1,)), ((), ())), preferred_element_type=F32)
        x = jnp.where(slot < limit, x, LOW)
        sco[b] = x
        ml[0:1] = jnp.maximum(ml[0:1], jnp.max(x, axis=0, keepdims=True))
        return 0

    def weigh(b, _):
        p = jnp.exp2((sco[b] - ml[0:1]) * SCALE2)
        ml[1:2] = ml[1:2] + jnp.sum(p, axis=0, keepdims=True)
        p = p.astype(BF)
        for h in range(HL):
            acc[:, 256 * h : 256 * h + 256] += dot(u_scr[b, DV * h : DV * h + DV], p[:, 256 * h : 256 * h + 256])
        return 0

    lax.fori_loop(0, 2 * NBLK, score, 0, unroll=2)
    pltpu.make_async_copy(u_ref, u_scr, usem).wait()
    lax.fori_loop(0, 2 * NBLK, weigh, 0, unroll=4)

    total = jnp.maximum(ml[1:2], 1.0)
    lse = ml[0:1] * SCALE2 + jnp.log2(total)
    res = (acc[...] * (1.0 / total)).T.astype(BF)
    for h in range(HL):
        out_ref[:, 16 * h : 16 * h + 16, :] = res[256 * h : 256 * h + 256].reshape(NX, 16, DV)
    hi = lse.astype(BF).astype(F32)
    mid = (lse - hi).astype(BF).astype(F32)
    low = lse - hi - mid
    for line in range(2):
        tail = [x[:, 256 * h + 128 * line : 256 * h + 128 * line + 128] for x in (hi, mid, low) for h in range(HL)]
        tail = jnp.concatenate(tail + tail[:4], axis=0).astype(BF)
        for a in range(8):
            out_ref[8 * line + a, CR : CR + 16, :] = tail


def attend(len0, len1, span, q, u, c0, c1):
    return pl.pallas_call(
        attend_kernel,
        out_shape=jax.ShapeDtypeStruct((NX, CR + 16, 128), BF),
        in_specs=[SM, SM, SM, VM, HB, HB, HB],
        out_specs=VM,
        scratch_shapes=[
            pltpu.VMEM((2 * NBLK, HL * DV, BLK), BF),
            pltpu.VMEM((2 * NBLK, WIDE, BLK), BF),
            pltpu.VMEM((ROWS, WIDE), BF),
            pltpu.VMEM((2 * NBLK, BLK, ROWS), F32),
            pltpu.VMEM((DV, ROWS), F32),
            pltpu.VMEM((8, ROWS), F32),
            pltpu.SemaphoreType.DMA((2 * NBLK,)),
            pltpu.SemaphoreType.DMA,
        ],
        compiler_params=pltpu.CompilerParams(vmem_limit_bytes=44 * 2**20),
        cost_estimate=pl.CostEstimate(flops=10**10, bytes_accessed=6 * 10**6, transcendentals=4 * 10**6),
    )(len0, len1, span, q, u, c0, c1)


def merge_kernel(x_ref, out_ref, scr):
    lines = []
    for k in range(2):
        lse = []
        for z in range(NX // 2):
            t = x_ref[2 * z + k, CR : CR + 16, :].astype(F32)
            lse.append(t[0:4] + t[4:8] + t[8:12])
        top = lse[0]
        for x in lse[1:]:
            top = jnp.maximum(top, x)
        wz = [jnp.exp2(x - top) for x in lse]
        scale = 1.0 / sum(wz)
        lines += [x * scale for x in wz]
    lines.append(jnp.zeros((128 - NX * HL, 128), F32))
    scr[...] = jnp.concatenate(lines, axis=0).T
    off = (2 * lax.axis_index("z") + lax.axis_index("core")) % 8 * TOK
    wt = scr[pl.ds(pl.multiple_of(off, TOK), TOK), :]
    merged = []
    for k in range(2):
        for h in range(HL):
            num = jnp.zeros((TOK, DV), F32)
            for z in range(NX // 2):
                at = (k * (NX // 2) + z) * HL + h
                num = num + wt[:, at : at + 1] * x_ref[2 * z + k, 16 * h : 16 * h + 16, :].astype(F32)
            merged.append(num.astype(BF))
    merged = jnp.concatenate(merged, axis=0)
    r, c = iota((128, 128), 0), iota((128, 128), 1)
    pick = (r // 8 == c % TOK) & (r % 8 == c // TOK)
    out_ref[...] = dot(jnp.where(pick, 1.0, 0.0).astype(BF), merged).astype(BF)


def merge(x):
    return pl.pallas_call(
        merge_kernel,
        out_shape=jax.ShapeDtypeStruct((TOK * 2 * HL, DV), BF),
        in_specs=[VM],
        out_specs=VM,
        scratch_shapes=[pltpu.VMEM((128, 128), F32)],
        compiler_params=pltpu.CompilerParams(vmem_limit_bytes=8 * 2**20),
        cost_estimate=pl.CostEstimate(flops=10**6, bytes_accessed=3 * 10**5, transcendentals=1000),
    )(x)


def body(queries, cache, cache_len, span_start, value_up):
    swap = [(0, 1), (1, 0)]
    mine = cache.T
    other = lax.ppermute(mine, "core", swap)
    other_len = lax.ppermute(cache_len, "core", swap)
    q = lax.all_to_all(pack(queries.transpose(0, 2, 1)), HEAD, split_axis=0, concat_axis=0, tiled=True)
    folded = pltpu.with_memory_space_constraint(fold(value_up, mine, other), pltpu.HBM)
    part = attend(cache_len, other_len, span_start, q, folded, mine, other)
    part = lax.all_to_all(part, CTX, split_axis=0, concat_axis=0, tiled=True)
    return merge(part).reshape(TOK, 2 * HL, DV)


def solution(mesh):
    fine = Mesh(mesh.devices.reshape(4, 4, 8, 2), ("y", "x", "z", "core"))
    placed = (P(HEAD, None, None), P(CTX, None), P(CTX), P(), P(HEAD, None, None))
    return jax.shard_map(body, mesh=fine, in_specs=placed, out_specs=P(CTX, HEAD, None), check_vma=False)
```

```python
import math

import jax
import jax.numpy as jnp
from jax import lax
from jax.experimental import pallas as pl
from jax.experimental.pallas import tpu as pltpu
from jax.sharding import Mesh, PartitionSpec as P

DC = 512
DR = 64
NOPE = 128
DV = 128
WIDE = DC + DR
HL = 4
TOK = 16
TG = 16 // HL
CR = TOK * HL
QR = CR * 9 // 2
NH = 16
NX = 16
SLOTS = 2048
ROWS = NH * CR
BLK = 1024
NBLK = SLOTS // BLK
SCALE2 = (NOPE + DR) ** (-0.5) * math.log2(math.e)
LOW = -1e30
BF = jnp.bfloat16
F32 = jnp.float32
VM = pl.BlockSpec(memory_space=pltpu.VMEM)
SM = pl.BlockSpec(memory_space=pltpu.SMEM)
HB = pl.BlockSpec(memory_space=pltpu.HBM)
GRANT = 119 * 2**19
HEAD = ("y", "x")
CTX = ("z", "core")


def dot(a, b):
    return jnp.dot(a, b, preferred_element_type=F32)


def iota(shape, dim):
    return lax.broadcasted_iota(jnp.int32, shape, dim)


def pack_kernel(q_ref, out_ref):
    shape = (NH * 16, TG * 128)
    r, c = iota(shape, 0), iota(shape, 1)
    head = 8 * (r // 16) + HL * lax.axis_index("core") + r % HL
    pick = ((r // HL) % TG == c // 128) & (head == c % 128)
    pick = jnp.where(pick, 1.0, 0.0).astype(BF)
    rot = []
    for t in range(2):
        x = jnp.concatenate([q_ref[TG * t + i] for i in range(TG)], axis=1)
        y = lax.dot_general(pick, x, (((1,), (1,)), ((), ())), preferred_element_type=F32).astype(BF)
        for j in range(4):
            out_ref[:, 32 * j + 16 * t : 32 * j + 16 * t + 16, :] = y[:, 128 * j : 128 * j + 128].reshape(NH, 16, 128)
        rot.append(y[:, DC:])
    out_ref[:, 128:144, :] = jnp.concatenate(rot, axis=1).reshape(NH, 16, 128)


def pack(q):
    return pl.pallas_call(
        pack_kernel,
        grid=(2,),
        out_shape=jax.ShapeDtypeStruct((NH, QR, 128), BF),
        in_specs=[pl.BlockSpec((2 * TG, WIDE, 128), lambda u: (u, 0, 0))],
        out_specs=pl.BlockSpec((NH, QR // 2, 128), lambda u: (0, u, 0)),
        compiler_params=pltpu.CompilerParams(vmem_limit_bytes=GRANT),
        cost_estimate=pl.CostEstimate(flops=10**9, bytes_accessed=4 * 10**6, transcendentals=0),
    )(q)


def fold_kernel(w_ref, c0, c1, out_ref):
    core = lax.axis_index("core")
    w = jnp.concatenate([w_ref[HL * core + h] for h in range(HL)], axis=1)
    for b in range(2 * NBLK):
        c = (c0, c1)[b // NBLK][0:DC, b % NBLK * BLK : b % NBLK * BLK + BLK]
        out_ref[b] = lax.dot_general(w, c, (((0,), (0,)), ((), ())), preferred_element_type=F32).astype(BF)


def fold(w, c0, c1):
    return pl.pallas_call(
        fold_kernel,
        out_shape=jax.ShapeDtypeStruct((2 * NBLK, HL * DV, BLK), BF),
        in_specs=[VM, VM, VM],
        out_specs=VM,
        compiler_params=pltpu.CompilerParams(vmem_limit_bytes=44 * 2**20),
        cost_estimate=pl.CostEstimate(flops=2 * 10**9, bytes_accessed=10**7, transcendentals=0),
    )(w, c0, c1)


def attend_kernel(len0, len1, span_ref, q_ref, u_ref, c0, c1, out_ref, u_scr, c_scr, qr, sco, acc, ml, sem, usem):
    core, span = lax.axis_index("core"), span_ref[0]
    shard = 2 * lax.axis_index("z") + core
    loads = [pltpu.make_async_copy(c, c_scr.at[s], sem.at[s]) for s, c in enumerate((c0, c1))]
    for c in loads:
        c.start()
    fetch = pltpu.make_async_copy(u_ref, u_scr, usem)

    r, c = iota((256, 256), 0), iota((256, 256), 1)
    pick = (r // 64 == c % HL) & (r // 16 % 4 == c // 64) & (r % 16 == c % 64 // HL)
    pick = jnp.where(pick, 1.0, 0.0).astype(BF)
    for g in range(NH // 4):
        x = q_ref[4 * g : 4 * g + 4]
        parts = [
            jnp.concatenate([x[:, 32 * j : 32 * j + 32], x[:, 144 + 32 * j : 176 + 32 * j]], axis=1).reshape(256, 128)
            for j in range(4)
        ]
        rot = [x[:, 144 * u + 128 : 144 * u + 144, DR * v : DR * v + DR] for u in range(2) for v in range(2)]
        parts.append(jnp.concatenate(rot, axis=1).reshape(256, DR))
        y = dot(pick, jnp.concatenate(parts, axis=1)).astype(BF)
        for h in range(HL):
            qr[256 * h + 64 * g : 256 * h + 64 * g + 64, :] = y[64 * h : 64 * h + 64]

    token = iota((1, ROWS), 1) % 256
    slot = iota((SLOTS, ROWS), 0)
    ml[0:1] = jnp.full((1, ROWS), LOW, F32)
    ml[1:2] = jnp.zeros((1, ROWS), F32)
    acc[...] = jnp.zeros_like(acc)

    def score(s, _):
        pltpu.make_async_copy(c0, c_scr.at[s], sem.at[s]).wait()

        @pl.when(s == 0)
        def _():
            fetch.start()

        filled = jnp.where(s == 0, len0[0], len1[0])
        first = jnp.where(s == 0, shard, shard + 1 - 2 * core) * SLOTS
        limit = jnp.minimum(filled, span + 1 + token - first)
        x = lax.dot_general(c_scr[s], qr[...], (((0,), (1,)), ((), ())), preferred_element_type=F32)
        x = jnp.where(slot < limit, x, LOW)
        for b in range(NBLK):
            sco[NBLK * s + b] = x[BLK * b : BLK * b + BLK]
        ml[0:1] = jnp.maximum(ml[0:1], jnp.max(x, axis=0, keepdims=True))
        return 0

    def weigh(b, _):
        p = jnp.exp2((sco[b] - ml[0:1]) * SCALE2)
        ml[1:2] = ml[1:2] + jnp.sum(p, axis=0, keepdims=True)
        p = p.astype(BF)
        for h in range(HL):
            acc[:, 256 * h : 256 * h + 256] += dot(u_scr[b, DV * h : DV * h + DV], p[:, 256 * h : 256 * h + 256])
        return 0

    lax.fori_loop(0, 2, score, 0)
    fetch.wait()
    lax.fori_loop(0, 2 * NBLK, weigh, 0, unroll=4)

    total = jnp.maximum(ml[1:2], 1.0)
    lse = ml[0:1] * SCALE2 + jnp.log2(total)
    res = (acc[...] * (1.0 / total)).T.astype(BF)
    for h in range(HL):
        out_ref[:, 16 * h : 16 * h + 16, :] = res[256 * h : 256 * h + 256].reshape(NX, 16, DV)
    hi = lse.astype(BF).astype(F32)
    mid = (lse - hi).astype(BF).astype(F32)
    low = lse - hi - mid
    for line in range(2):
        tail = [x[:, 256 * h + 128 * line : 256 * h + 128 * line + 128] for x in (hi, mid, low) for h in range(HL)]
        tail = jnp.concatenate(tail + tail[:4], axis=0).astype(BF)
        for a in range(8):
            out_ref[8 * line + a, CR : CR + 16, :] = tail


def attend(len0, len1, span, q, u, c0, c1):
    return pl.pallas_call(
        attend_kernel,
        out_shape=jax.ShapeDtypeStruct((NX, CR + 16, 128), BF),
        in_specs=[SM, SM, SM, VM, HB, HB, HB],
        out_specs=VM,
        scratch_shapes=[
            pltpu.VMEM((2 * NBLK, HL * DV, BLK), BF),
            pltpu.VMEM((2, WIDE, SLOTS), BF),
            pltpu.VMEM((ROWS, WIDE), BF),
            pltpu.VMEM((2 * NBLK, BLK, ROWS), F32),
            pltpu.VMEM((DV, ROWS), F32),
            pltpu.VMEM((8, ROWS), F32),
            pltpu.SemaphoreType.DMA((2,)),
            pltpu.SemaphoreType.DMA,
        ],
        compiler_params=pltpu.CompilerParams(vmem_limit_bytes=44 * 2**20),
        cost_estimate=pl.CostEstimate(flops=10**10, bytes_accessed=6 * 10**6, transcendentals=4 * 10**6),
    )(len0, len1, span, q, u, c0, c1)


def merge_kernel(x_ref, out_ref, scr):
    lines = []
    for k in range(2):
        lse = []
        for z in range(NX // 2):
            t = x_ref[2 * z + k, CR : CR + 16, :].astype(F32)
            lse.append(t[0:4] + t[4:8] + t[8:12])
        top = lse[0]
        for x in lse[1:]:
            top = jnp.maximum(top, x)
        wz = [jnp.exp2(x - top) for x in lse]
        scale = 1.0 / sum(wz)
        lines += [x * scale for x in wz]
    lines.append(jnp.zeros((128 - NX * HL, 128), F32))
    scr[...] = jnp.concatenate(lines, axis=0).T
    off = (2 * lax.axis_index("z") + lax.axis_index("core")) % 8 * TOK
    wt = scr[pl.ds(pl.multiple_of(off, TOK), TOK), :]
    merged = []
    for k in range(2):
        for h in range(HL):
            num = jnp.zeros((TOK, DV), F32)
            for z in range(NX // 2):
                at = (k * (NX // 2) + z) * HL + h
                num = num + wt[:, at : at + 1] * x_ref[2 * z + k, 16 * h : 16 * h + 16, :].astype(F32)
            merged.append(num.astype(BF))
    merged = jnp.concatenate(merged, axis=0)
    r, c = iota((128, 128), 0), iota((128, 128), 1)
    pick = (r // 8 == c % TOK) & (r % 8 == c // TOK)
    out_ref[...] = dot(jnp.where(pick, 1.0, 0.0).astype(BF), merged).astype(BF)


def merge(x):
    return pl.pallas_call(
        merge_kernel,
        out_shape=jax.ShapeDtypeStruct((TOK * 2 * HL, DV), BF),
        in_specs=[VM],
        out_specs=VM,
        scratch_shapes=[pltpu.VMEM((128, 128), F32)],
        compiler_params=pltpu.CompilerParams(vmem_limit_bytes=8 * 2**20),
        cost_estimate=pl.CostEstimate(flops=10**6, bytes_accessed=3 * 10**5, transcendentals=1000),
    )(x)


def body(queries, cache, cache_len, span_start, value_up):
    swap = [(0, 1), (1, 0)]
    mine = cache.T
    other = lax.ppermute(mine, "core", swap)
    other_len = lax.ppermute(cache_len, "core", swap)
    q = lax.all_to_all(pack(queries.transpose(0, 2, 1)), HEAD, split_axis=0, concat_axis=0, tiled=True)
    folded = pltpu.with_memory_space_constraint(fold(value_up, mine, other), pltpu.HBM)
    part = attend(cache_len, other_len, span_start, q, folded, mine, other)
    part = lax.all_to_all(part, CTX, split_axis=0, concat_axis=0, tiled=True)
    return merge(part).reshape(TOK, 2 * HL, DV)


def solution(mesh):
    fine = Mesh(mesh.devices.reshape(4, 4, 8, 2), ("y", "x", "z", "core"))
    placed = (P(HEAD, None, None), P(CTX, None), P(CTX), P(), P(HEAD, None, None))
    return jax.shard_map(body, mesh=fine, in_specs=placed, out_specs=P(CTX, HEAD, None), check_vma=False)
```

```python
import math

import jax
import jax.numpy as jnp
from jax import lax
from jax.experimental import pallas as pl
from jax.experimental.pallas import tpu as pltpu
from jax.sharding import Mesh, PartitionSpec as P

DC = 512
DR = 64
NOPE = 128
DV = 128
WIDE = DC + DR
HL = 4
TOK = 16
TG = 16 // HL
CR = TOK * HL
QR = CR * 9 // 2
NH = 16
NX = 16
SLOTS = 2048
ROWS = NH * CR
BLK = 1024
NBLK = SLOTS // BLK
SCALE2 = (NOPE + DR) ** (-0.5) * math.log2(math.e)
LOW = -1e30
BF = jnp.bfloat16
F32 = jnp.float32
VM = pl.BlockSpec(memory_space=pltpu.VMEM)
SM = pl.BlockSpec(memory_space=pltpu.SMEM)
HB = pl.BlockSpec(memory_space=pltpu.HBM)
GRANT = 119 * 2**19
HEAD = ("y", "x")
CTX = ("z", "core")


def dot(a, b):
    return jnp.dot(a, b, preferred_element_type=F32)


def iota(shape, dim):
    return lax.broadcasted_iota(jnp.int32, shape, dim)


def pack_kernel(q0, q1, out_ref):
    shape = (NH * 16, TG * 128)
    r, c = iota(shape, 0), iota(shape, 1)
    head = 8 * (r // 16) + HL * lax.axis_index("core") + r % HL
    pick = ((r // HL) % TG == c // 128) & (head == c % 128)
    pick = jnp.where(pick, 1.0, 0.0).astype(BF)
    rot = []
    for t in range(2):
        x = jnp.concatenate([(q0, q1)[t][i] for i in range(TG)], axis=1)
        y = lax.dot_general(pick, x, (((1,), (1,)), ((), ())), preferred_element_type=F32).astype(BF)
        for j in range(4):
            out_ref[:, 32 * j + 16 * t : 32 * j + 16 * t + 16, :] = y[:, 128 * j : 128 * j + 128].reshape(NH, 16, 128)
        rot.append(y[:, DC:])
    out_ref[:, 128:144, :] = jnp.concatenate(rot, axis=1).reshape(NH, 16, 128)


def pack(q):
    return pl.pallas_call(
        pack_kernel,
        grid=(2,),
        out_shape=jax.ShapeDtypeStruct((NH, QR, 128), BF),
        in_specs=[pl.BlockSpec((TG, WIDE, 128), lambda u: (2 * u, 0, 0)), pl.BlockSpec((TG, WIDE, 128), lambda u: (2 * u + 1, 0, 0))],
        out_specs=pl.BlockSpec((NH, QR // 2, 128), lambda u: (0, u, 0)),
        compiler_params=pltpu.CompilerParams(vmem_limit_bytes=GRANT),
        cost_estimate=pl.CostEstimate(flops=10**9, bytes_accessed=4 * 10**6, transcendentals=0),
    )(q, q)


def fold_kernel(w_ref, c0, c1, out_ref):
    core = lax.axis_index("core")
    w = jnp.concatenate([w_ref[HL * core + h] for h in range(HL)], axis=1)
    for b in range(2 * NBLK):
        c = (c0, c1)[b // NBLK][0:DC, b % NBLK * BLK : b % NBLK * BLK + BLK]
        out_ref[b] = lax.dot_general(w, c, (((0,), (0,)), ((), ())), preferred_element_type=F32).astype(BF)


def fold(w, c0, c1):
    return pl.pallas_call(
        fold_kernel,
        out_shape=jax.ShapeDtypeStruct((2 * NBLK, HL * DV, BLK), BF),
        in_specs=[VM, VM, VM],
        out_specs=VM,
        compiler_params=pltpu.CompilerParams(vmem_limit_bytes=44 * 2**20),
        cost_estimate=pl.CostEstimate(flops=2 * 10**9, bytes_accessed=10**7, transcendentals=0),
    )(w, c0, c1)


def attend_kernel(len0, len1, span_ref, q_ref, u_ref, c0, c1, out_ref, u_scr, c_scr, qr, sco, acc, ml, sem, usem):
    core, span = lax.axis_index("core"), span_ref[0]
    shard = 2 * lax.axis_index("z") + core
    loads = [pltpu.make_async_copy(c, c_scr.at[s], sem.at[s]) for s, c in enumerate((c0, c1))]
    for c in loads:
        c.start()
    fetch = pltpu.make_async_copy(u_ref, u_scr, usem)

    r, c = iota((256, 256), 0), iota((256, 256), 1)
    pick = (r // 64 == c % HL) & (r // 16 % 4 == c // 64) & (r % 16 == c % 64 // HL)
    pick = jnp.where(pick, 1.0, 0.0).astype(BF)
    for g in range(NH // 4):
        x = q_ref[4 * g : 4 * g + 4]
        parts = [
            jnp.concatenate([x[:, 32 * j : 32 * j + 32], x[:, 144 + 32 * j : 176 + 32 * j]], axis=1).reshape(256, 128)
            for j in range(4)
        ]
        rot = [x[:, 144 * u + 128 : 144 * u + 144, DR * v : DR * v + DR] for u in range(2) for v in range(2)]
        parts.append(jnp.concatenate(rot, axis=1).reshape(256, DR))
        y = dot(pick, jnp.concatenate(parts, axis=1)).astype(BF)
        for h in range(HL):
            qr[256 * h + 64 * g : 256 * h + 64 * g + 64, :] = y[64 * h : 64 * h + 64]

    token = iota((1, ROWS), 1) % 256
    slot = iota((SLOTS, ROWS), 0)
    ml[0:1] = jnp.full((1, ROWS), LOW, F32)
    ml[1:2] = jnp.zeros((1, ROWS), F32)
    acc[...] = jnp.zeros_like(acc)

    def score(s, _):
        pltpu.make_async_copy(c0, c_scr.at[s], sem.at[s]).wait()

        @pl.when(s == 0)
        def _():
            fetch.start()

        filled = jnp.where(s == 0, len0[0], len1[0])
        first = jnp.where(s == 0, shard, shard + 1 - 2 * core) * SLOTS
        limit = jnp.minimum(filled, span + 1 + token - first)
        x = lax.dot_general(c_scr[s], qr[...], (((0,), (1,)), ((), ())), preferred_element_type=F32)
        x = jnp.where(slot < limit, x, LOW)
        for b in range(NBLK):
            sco[NBLK * s + b] = x[BLK * b : BLK * b + BLK]
        ml[0:1] = jnp.maximum(ml[0:1], jnp.max(x, axis=0, keepdims=True))
        return 0

    def weigh(b, _):
        p = jnp.exp2((sco[b] - ml[0:1]) * SCALE2)
        ml[1:2] = ml[1:2] + jnp.sum(p, axis=0, keepdims=True)
        p = p.astype(BF)
        for h in range(HL):
            acc[:, 256 * h : 256 * h + 256] += dot(u_scr[b, DV * h : DV * h + DV], p[:, 256 * h : 256 * h + 256])
        return 0

    lax.fori_loop(0, 2, score, 0)
    fetch.wait()
    lax.fori_loop(0, 2 * NBLK, weigh, 0, unroll=4)

    total = jnp.maximum(ml[1:2], 1.0)
    lse = ml[0:1] * SCALE2 + jnp.log2(total)
    res = (acc[...] * (1.0 / total)).T.astype(BF)
    for h in range(HL):
        out_ref[:, 16 * h : 16 * h + 16, :] = res[256 * h : 256 * h + 256].reshape(NX, 16, DV)
    hi = lse.astype(BF).astype(F32)
    mid = (lse - hi).astype(BF).astype(F32)
    low = lse - hi - mid
    for line in range(2):
        tail = [x[:, 256 * h + 128 * line : 256 * h + 128 * line + 128] for x in (hi, mid, low) for h in range(HL)]
        tail = jnp.concatenate(tail + tail[:4], axis=0).astype(BF)
        for a in range(8):
            out_ref[8 * line + a, CR : CR + 16, :] = tail


def attend(len0, len1, span, q, u, c0, c1):
    return pl.pallas_call(
        attend_kernel,
        out_shape=jax.ShapeDtypeStruct((NX, CR + 16, 128), BF),
        in_specs=[SM, SM, SM, VM, HB, HB, HB],
        out_specs=VM,
        scratch_shapes=[
            pltpu.VMEM((2 * NBLK, HL * DV, BLK), BF),
            pltpu.VMEM((2, WIDE, SLOTS), BF),
            pltpu.VMEM((ROWS, WIDE), BF),
            pltpu.VMEM((2 * NBLK, BLK, ROWS), F32),
            pltpu.VMEM((DV, ROWS), F32),
            pltpu.VMEM((8, ROWS), F32),
            pltpu.SemaphoreType.DMA((2,)),
            pltpu.SemaphoreType.DMA,
        ],
        compiler_params=pltpu.CompilerParams(vmem_limit_bytes=44 * 2**20),
        cost_estimate=pl.CostEstimate(flops=10**10, bytes_accessed=6 * 10**6, transcendentals=4 * 10**6),
    )(len0, len1, span, q, u, c0, c1)


def merge_kernel(x_ref, out_ref, scr):
    lines = []
    for k in range(2):
        lse = []
        for z in range(NX // 2):
            t = x_ref[2 * z + k, CR : CR + 16, :].astype(F32)
            lse.append(t[0:4] + t[4:8] + t[8:12])
        top = lse[0]
        for x in lse[1:]:
            top = jnp.maximum(top, x)
        wz = [jnp.exp2(x - top) for x in lse]
        scale = 1.0 / sum(wz)
        lines += [x * scale for x in wz]
    lines.append(jnp.zeros((128 - NX * HL, 128), F32))
    scr[...] = jnp.concatenate(lines, axis=0).T
    off = (2 * lax.axis_index("z") + lax.axis_index("core")) % 8 * TOK
    wt = scr[pl.ds(pl.multiple_of(off, TOK), TOK), :]
    merged = []
    for k in range(2):
        for h in range(HL):
            num = jnp.zeros((TOK, DV), F32)
            for z in range(NX // 2):
                at = (k * (NX // 2) + z) * HL + h
                num = num + wt[:, at : at + 1] * x_ref[2 * z + k, 16 * h : 16 * h + 16, :].astype(F32)
            merged.append(num.astype(BF))
    merged = jnp.concatenate(merged, axis=0)
    r, c = iota((128, 128), 0), iota((128, 128), 1)
    pick = (r // 8 == c % TOK) & (r % 8 == c // TOK)
    out_ref[...] = dot(jnp.where(pick, 1.0, 0.0).astype(BF), merged).astype(BF)


def merge(x):
    return pl.pallas_call(
        merge_kernel,
        out_shape=jax.ShapeDtypeStruct((TOK * 2 * HL, DV), BF),
        in_specs=[VM],
        out_specs=VM,
        scratch_shapes=[pltpu.VMEM((128, 128), F32)],
        compiler_params=pltpu.CompilerParams(vmem_limit_bytes=8 * 2**20),
        cost_estimate=pl.CostEstimate(flops=10**6, bytes_accessed=3 * 10**5, transcendentals=1000),
    )(x)


def body(queries, cache, cache_len, span_start, value_up):
    swap = [(0, 1), (1, 0)]
    mine = cache.T
    other = lax.ppermute(mine, "core", swap)
    other_len = lax.ppermute(cache_len, "core", swap)
    q = lax.all_to_all(pack(queries.transpose(0, 2, 1)), HEAD, split_axis=0, concat_axis=0, tiled=True)
    folded = pltpu.with_memory_space_constraint(fold(value_up, mine, other), pltpu.HBM)
    part = attend(cache_len, other_len, span_start, q, folded, mine, other)
    part = lax.all_to_all(part, CTX, split_axis=0, concat_axis=0, tiled=True)
    return merge(part).reshape(TOK, 2 * HL, DV)


def solution(mesh):
    fine = Mesh(mesh.devices.reshape(4, 4, 8, 2), ("y", "x", "z", "core"))
    placed = (P(HEAD, None, None), P(CTX, None), P(CTX), P(), P(HEAD, None, None))
    return jax.shard_map(body, mesh=fine, in_specs=placed, out_specs=P(CTX, HEAD, None), check_vma=False)
```

```python
import math

import jax
import jax.numpy as jnp
from jax import lax
from jax.experimental import pallas as pl
from jax.experimental.pallas import tpu as pltpu
from jax.sharding import Mesh, PartitionSpec as P

DC = 512
DR = 64
NOPE = 128
DV = 128
WIDE = DC + DR
HL = 4
TOK = 16
TG = 16 // HL
CR = TOK * HL
QR = CR * 9 // 2
NH = 16
NX = 16
SLOTS = 2048
ROWS = NH * CR
BLK = 1024
NBLK = SLOTS // BLK
SCALE2 = (NOPE + DR) ** (-0.5) * math.log2(math.e)
LOW = -1e30
BF = jnp.bfloat16
F32 = jnp.float32
VM = pl.BlockSpec(memory_space=pltpu.VMEM)
SM = pl.BlockSpec(memory_space=pltpu.SMEM)
HB = pl.BlockSpec(memory_space=pltpu.HBM)
GRANT = 119 * 2**19
HEAD = ("y", "x")
CTX = ("z", "core")


def dot(a, b):
    return jnp.dot(a, b, preferred_element_type=F32)


def iota(shape, dim):
    return lax.broadcasted_iota(jnp.int32, shape, dim)


def pack_kernel(q0, q1, out_ref):
    shape = (NH * 16, TG * 128)
    r, c = iota(shape, 0), iota(shape, 1)
    head = 8 * (r // 16) + HL * lax.axis_index("core") + r % HL
    pick = ((r // HL) % TG == c // 128) & (head == c % 128)
    pick = jnp.where(pick, 1.0, 0.0).astype(BF)
    rot = []
    for t in range(2):
        x = jnp.concatenate([(q0, q1)[t][i] for i in range(TG)], axis=1)
        y = lax.dot_general(pick, x, (((1,), (1,)), ((), ())), preferred_element_type=F32).astype(BF)
        for j in range(4):
            out_ref[:, 32 * j + 16 * t : 32 * j + 16 * t + 16, :] = y[:, 128 * j : 128 * j + 128].reshape(NH, 16, 128)
        rot.append(y[:, DC:])
    out_ref[:, 128:144, :] = jnp.concatenate(rot, axis=1).reshape(NH, 16, 128)


def pack(q):
    return pl.pallas_call(
        pack_kernel,
        grid=(2,),
        out_shape=jax.ShapeDtypeStruct((NH, QR, 128), BF),
        in_specs=[pl.BlockSpec((TG, WIDE, 128), lambda u: (2 * u, 0, 0)), pl.BlockSpec((TG, WIDE, 128), lambda u: (2 * u + 1, 0, 0))],
        out_specs=pl.BlockSpec((NH, QR // 2, 128), lambda u: (0, u, 0)),
        compiler_params=pltpu.CompilerParams(vmem_limit_bytes=GRANT),
        cost_estimate=pl.CostEstimate(flops=10**9, bytes_accessed=4 * 10**6, transcendentals=0),
    )(q, q)


def fold_kernel(w_ref, c0, c1, out_ref):
    core = lax.axis_index("core")
    w = jnp.concatenate([w_ref[HL * core + h] for h in range(HL)], axis=1)
    for b in range(2 * NBLK):
        c = (c0, c1)[b // NBLK][0:DC, b % NBLK * BLK : b % NBLK * BLK + BLK]
        out_ref[b] = lax.dot_general(w, c, (((0,), (0,)), ((), ())), preferred_element_type=F32).astype(BF)


def fold(w, c0, c1):
    return pl.pallas_call(
        fold_kernel,
        out_shape=jax.ShapeDtypeStruct((2 * NBLK, HL * DV, BLK), BF),
        in_specs=[VM, VM, VM],
        out_specs=VM,
        compiler_params=pltpu.CompilerParams(vmem_limit_bytes=44 * 2**20),
        cost_estimate=pl.CostEstimate(flops=2 * 10**9, bytes_accessed=10**7, transcendentals=0),
    )(w, c0, c1)


def attend_kernel(len0, len1, span_ref, q_ref, u_ref, c0, c1, out_ref, u_scr, c_scr, qr, sco, acc, ml, sem, usem):
    core, span = lax.axis_index("core"), span_ref[0]
    shard = 2 * lax.axis_index("z") + core
    loads = [pltpu.make_async_copy(c, c_scr.at[s], sem.at[s]) for s, c in enumerate((c0, c1))]
    for c in loads:
        c.start()
    fetch = pltpu.make_async_copy(u_ref, u_scr, usem)

    r, c = iota((256, 256), 0), iota((256, 256), 1)
    pick = (r // 64 == c % HL) & (r // 16 % 4 == c // 64) & (r % 16 == c % 64 // HL)
    pick = jnp.where(pick, 1.0, 0.0).astype(BF)
    for g in range(NH // 4):
        x = q_ref[4 * g : 4 * g + 4]
        parts = [
            jnp.concatenate([x[:, 32 * j : 32 * j + 32], x[:, 144 + 32 * j : 176 + 32 * j]], axis=1).reshape(256, 128)
            for j in range(4)
        ]
        rot = [x[:, 144 * u + 128 : 144 * u + 144, DR * v : DR * v + DR] for u in range(2) for v in range(2)]
        parts.append(jnp.concatenate(rot, axis=1).reshape(256, DR))
        y = dot(pick, jnp.concatenate(parts, axis=1)).astype(BF)
        for h in range(HL):
            qr[256 * h + 64 * g : 256 * h + 64 * g + 64, :] = y[64 * h : 64 * h + 64]

    token = iota((1, ROWS), 1) % 256
    slot = iota((SLOTS, ROWS), 0)
    ml[0:1] = jnp.full((1, ROWS), LOW, F32)

    def score(s, _):
        pltpu.make_async_copy(c0, c_scr.at[s], sem.at[s]).wait()

        @pl.when(s == 0)
        def _():
            fetch.start()

        filled = jnp.where(s == 0, len0[0], len1[0])
        first = jnp.where(s == 0, shard, shard + 1 - 2 * core) * SLOTS
        limit = jnp.minimum(filled, span + 1 + token - first)
        x = lax.dot_general(c_scr[s], qr[...], (((0,), (1,)), ((), ())), preferred_element_type=F32)
        x = jnp.where(slot < limit, x, LOW)
        for b in range(NBLK):
            sco[NBLK * s + b] = x[BLK * b : BLK * b + BLK]
        ml[0:1] = jnp.maximum(ml[0:1], jnp.max(x, axis=0, keepdims=True))
        return 0

    lax.fori_loop(0, 2, score, 0)
    fetch.wait()
    total = 0.0
    for b in range(2 * NBLK):
        p = jnp.exp2((sco[b] - ml[0:1]) * SCALE2)
        total = total + jnp.sum(p, axis=0, keepdims=True)
        p = p.astype(BF)
        for h in range(HL):
            cols = slice(256 * h, 256 * h + 256)
            up = dot(u_scr[b, DV * h : DV * h + DV], p[:, cols])
            acc[:, cols] = up if b == 0 else acc[:, cols] + up

    total = jnp.maximum(total, 1.0)
    lse = ml[0:1] * SCALE2 + jnp.log2(total)
    res = (acc[...] * (1.0 / total)).T.astype(BF)
    for h in range(HL):
        out_ref[:, 16 * h : 16 * h + 16, :] = res[256 * h : 256 * h + 256].reshape(NX, 16, DV)
    hi = lse.astype(BF).astype(F32)
    mid = (lse - hi).astype(BF).astype(F32)
    low = lse - hi - mid
    for line in range(2):
        tail = [x[:, 256 * h + 128 * line : 256 * h + 128 * line + 128] for x in (hi, mid, low) for h in range(HL)]
        tail = jnp.concatenate(tail + tail[:4], axis=0).astype(BF)
        for a in range(8):
            out_ref[8 * line + a, CR : CR + 16, :] = tail


def attend(len0, len1, span, q, u, c0, c1):
    return pl.pallas_call(
        attend_kernel,
        out_shape=jax.ShapeDtypeStruct((NX, CR + 16, 128), BF),
        in_specs=[SM, SM, SM, VM, HB, HB, HB],
        out_specs=VM,
        scratch_shapes=[
            pltpu.VMEM((2 * NBLK, HL * DV, BLK), BF),
            pltpu.VMEM((2, WIDE, SLOTS), BF),
            pltpu.VMEM((ROWS, WIDE), BF),
            pltpu.VMEM((2 * NBLK, BLK, ROWS), F32),
            pltpu.VMEM((DV, ROWS), F32),
            pltpu.VMEM((8, ROWS), F32),
            pltpu.SemaphoreType.DMA((2,)),
            pltpu.SemaphoreType.DMA,
        ],
        compiler_params=pltpu.CompilerParams(vmem_limit_bytes=44 * 2**20),
        cost_estimate=pl.CostEstimate(flops=10**10, bytes_accessed=6 * 10**6, transcendentals=4 * 10**6),
    )(len0, len1, span, q, u, c0, c1)


def merge_kernel(x_ref, out_ref, scr):
    lines = []
    for k in range(2):
        lse = []
        for z in range(NX // 2):
            t = x_ref[2 * z + k, CR : CR + 16, :].astype(F32)
            lse.append(t[0:4] + t[4:8] + t[8:12])
        top = lse[0]
        for x in lse[1:]:
            top = jnp.maximum(top, x)
        wz = [jnp.exp2(x - top) for x in lse]
        scale = 1.0 / sum(wz)
        lines += [x * scale for x in wz]
    lines.append(jnp.zeros((128 - NX * HL, 128), F32))
    scr[...] = jnp.concatenate(lines, axis=0).T
    off = (2 * lax.axis_index("z") + lax.axis_index("core")) % 8 * TOK
    wt = scr[pl.ds(pl.multiple_of(off, TOK), TOK), :]
    merged = []
    for k in range(2):
        for h in range(HL):
            num = jnp.zeros((TOK, DV), F32)
            for z in range(NX // 2):
                at = (k * (NX // 2) + z) * HL + h
                num = num + wt[:, at : at + 1] * x_ref[2 * z + k, 16 * h : 16 * h + 16, :].astype(F32)
            merged.append(num.astype(BF))
    merged = jnp.concatenate(merged, axis=0)
    r, c = iota((128, 128), 0), iota((128, 128), 1)
    pick = (r // 8 == c % TOK) & (r % 8 == c // TOK)
    out_ref[...] = dot(jnp.where(pick, 1.0, 0.0).astype(BF), merged).astype(BF)


def merge(x):
    return pl.pallas_call(
        merge_kernel,
        out_shape=jax.ShapeDtypeStruct((TOK * 2 * HL, DV), BF),
        in_specs=[VM],
        out_specs=VM,
        scratch_shapes=[pltpu.VMEM((128, 128), F32)],
        compiler_params=pltpu.CompilerParams(vmem_limit_bytes=8 * 2**20),
        cost_estimate=pl.CostEstimate(flops=10**6, bytes_accessed=3 * 10**5, transcendentals=1000),
    )(x)


def body(queries, cache, cache_len, span_start, value_up):
    swap = [(0, 1), (1, 0)]
    mine = cache.T
    other = lax.ppermute(mine, "core", swap)
    other_len = lax.ppermute(cache_len, "core", swap)
    q = lax.all_to_all(pack(queries.transpose(0, 2, 1)), HEAD, split_axis=0, concat_axis=0, tiled=True)
    folded = pltpu.with_memory_space_constraint(fold(value_up, mine, other), pltpu.HBM)
    part = attend(cache_len, other_len, span_start, q, folded, mine, other)
    part = lax.all_to_all(part, CTX, split_axis=0, concat_axis=0, tiled=True)
    return merge(part).reshape(TOK, 2 * HL, DV)


def solution(mesh):
    fine = Mesh(mesh.devices.reshape(4, 4, 8, 2), ("y", "x", "z", "core"))
    placed = (P(HEAD, None, None), P(CTX, None), P(CTX), P(), P(HEAD, None, None))
    return jax.shard_map(body, mesh=fine, in_specs=placed, out_specs=P(CTX, HEAD, None), check_vma=False)
```
